128 devices in a mesh: seq: 128 (over x, z, y, core).
Axes of the slice: x: 4, y: 4, z: 4, core: 2. Of those that a mesh axis runs over, the one named last changes fastest.
Arguments:
- tokens: bfloat16 [16384, 1024], P('seq'), may hold values from -24 to 24
- grad_out: bfloat16 [16384, 1024], P('seq'), may hold values from -24 to 24
- w_in: bfloat16 [1024, 4096], replicated, may hold values from -0.1875 to 0.1875
- w_out: bfloat16 [1024, 1024], replicated, may hold values from -0.1875 to 0.1875
- rel_bias: float32 [8, 16], replicated, may hold values from -4 to 4
- send_rows: int32 [128, 128], P('seq'), may hold values from 0 to 127, each once within a row
- recv_place: int32 [128, 128], P('seq'), may hold values from 0 to 127, each once within a row
- block_first: int32 [128], P('seq'), may hold values from 0 to 0, as said below
- user_rows: int32 [128], P('seq'), may hold values from 1 to 128, as said below
- stamps: int32 [16384], P('seq'), may hold values from 0 to 12160, as said below
Outputs:
- out: bfloat16 [16384, 1024], P('seq')
- grad_x: bfloat16 [16384, 1024], P('seq')
- grad_w1: float32 [1024, 4096], P('seq')
- grad_w2: float32 [1024, 1024], P('seq')
The draws below stay inside these ranges and needn't reach their ends.
Inputs may be any that keep to these rules, and one draw needn't show every extreme that they name: Loader l sends its row send_rows[l, o] to owner o: every owner receives exactly 1 row from every loader. In each owner's row, a permutation: recv_place[o, s] = l + c names the c-th row that loader l sends to owner o. `block_first`: an index among one owner's 1 block; each user holds consecutive blocks of one owner, and an owner's block 0 starts a user. `user_rows`: equal over the blocks of one user, and between (128 times (the user's blocks - 1)) + 1 and 128 times its blocks; some owner holds a single user of 128 rows. `stamps`: never falling along one owner's row slots.
All inputs are finite; a program needn't handle non-finite values.
Results may differ from the reference program's by a relative error of at most 0.0068.
Values may be sent and summed in bfloat16 or wider, within the bound.
A program may use at most 128 MiB of HBM per device.

```python
import jax
import jax.numpy as jnp
from jax import lax

D = 1024
HEADS = 8
BLOCK = 128
NBUCK = 16
TOK_DEV = 128
BLOCKS_DEV = 1
TOKENS = 16384
N_SEQ = 128


def user_layout(key):
    starts = jax.random.randint(jax.random.fold_in(key, 11), (N_SEQ, BLOCKS_DEV), 0, 2)
    full_owner = jax.random.randint(jax.random.fold_in(key, 12), (), 0, N_SEQ)
    split_owner = (full_owner + 1) % N_SEQ
    index = jnp.arange(BLOCKS_DEV, dtype=jnp.int32)[None, :]
    owner = jnp.arange(N_SEQ, dtype=jnp.int32)[:, None]
    starts = jnp.where((owner == split_owner) & (index == BLOCKS_DEV - 1), 1, starts)
    starts = jnp.where(owner == full_owner, 0, starts)
    starts = jnp.where(index == 0, 1, starts)
    first = lax.cummax(jnp.where(starts == 1, index, 0), axis=1)
    begin = jnp.where(starts == 1, index, BLOCKS_DEV)
    later = jnp.concatenate([begin[:, 1:], jnp.full((N_SEQ, 1), BLOCKS_DEV, jnp.int32)], axis=1)
    ends = lax.cummin(later, axis=1, reverse=True)
    extra = jax.random.randint(jax.random.fold_in(key, 13), (N_SEQ, BLOCKS_DEV), 1, BLOCK + 1)
    extra = jnp.take_along_axis(extra, first, axis=1)
    extra = jnp.where(owner == full_owner, BLOCK, extra)
    rows = (ends - first - 1) * BLOCK + extra
    return (first.astype(jnp.int32), rows.astype(jnp.int32))


def draw_block_first(key, part):
    first, rows = user_layout(key)
    return first.reshape(-1)


def draw_user_rows(key, part):
    first, rows = user_layout(key)
    return rows.reshape(-1)


def draw_stamps(key, part):
    key = jax.random.fold_in(key, 5)
    steps_between = jax.random.randint(key, (N_SEQ, TOK_DEV), 0, 96)
    times = jnp.cumsum(steps_between, axis=1).astype(jnp.int32)
    top_owner = jax.random.randint(jax.random.fold_in(key, 6), (), 0, N_SEQ)
    owner = jnp.arange(N_SEQ, dtype=jnp.int32)[:, None]
    index = jnp.arange(TOK_DEV, dtype=jnp.int32)[None, :]
    times = jnp.where((owner == top_owner) & (index == TOK_DEV - 1), 95 * TOK_DEV, times)
    return times.astype(jnp.int32).reshape(-1)


def spiked(values, key, source, target, parts, factor):
    owner, partner = [(jnp.arange(values.shape[position]) // (values.shape[position] // parts)).reshape([-1 if axis == position else 1 for axis in range(values.ndim)]) for position in (source, target)]
    chosen = jax.random.permutation(key, parts)[partner]
    strong = (owner == chosen) | (owner == (partner + parts // 2) % parts)
    return jnp.where(strong, factor * values, values)


def levels(own_key, shape, split, least, top_value):
    gain, own = 1.0, jax.random.fold_in(own_key, 6)
    for dim, blocks in split:
        draws = jnp.exp(jax.random.uniform(jax.random.fold_in(own, dim), (blocks,), jnp.float32, least / len(split), top_value / len(split)))
        gain = gain * jnp.repeat(draws, shape[dim] // blocks).reshape([-1 if axis == dim else 1 for axis in range(len(shape))])
    return gain


def gaussian(key, dims, scale, limit, pieces=(), kind=jnp.bfloat16):
    array = scale * jax.random.normal(key, dims, jnp.float32)
    if pieces:
        array = array * levels(key, dims, pieces, -0.22, 0.18)
    return jnp.clip(array, -limit, limit).astype(kind)


def heavy_noise(stream_key, dims, scale, most, pieces, heavy, kind=jnp.bfloat16):
    array = scale * jax.random.normal(stream_key, dims, jnp.float32)
    if pieces:
        array = array * levels(stream_key, dims, pieces, -0.22, 0.18)
    return jnp.clip(spiked(array, jax.random.fold_in(stream_key, 3), *heavy), -most, most).astype(kind)


def setup_inputs(seed: int = 0) -> dict:
    splits = jax.random.split(jax.random.key(seed), 11)
    tokens = heavy_noise(splits[0], (TOKENS, D), 1.0, 24.0, ((0, 128),), (0, 1, 128, 5.5))
    grad_out = heavy_noise(splits[1], (TOKENS, D), 1.0, 24.0, ((0, 128),), (0, 1, 128, 5.5))
    w_in = gaussian(splits[2], (D, 4 * D), D ** -0.5, 0.1875)
    w_out = gaussian(splits[3], (D, D), D ** -0.5, 0.1875)
    rel_bias = gaussian(splits[4], (HEADS, NBUCK), 1.0, 4.0, (), jnp.float32)
    send_rows = jax.vmap(lambda own: jax.random.permutation(own, TOK_DEV))(jax.random.split(splits[5], N_SEQ)).reshape((N_SEQ, TOK_DEV)).astype(jnp.int32)
    recv_place = jax.vmap(lambda own: jax.random.permutation(own, TOK_DEV))(jax.random.split(splits[6], N_SEQ)).reshape((N_SEQ, TOK_DEV)).astype(jnp.int32)
    block_first = draw_block_first(jax.random.fold_in(splits[10], 71), 0)
    user_rows = draw_user_rows(jax.random.fold_in(splits[10], 71), 0)
    stamps = draw_stamps(jax.random.fold_in(splits[10], 71), 0)
    return {"tokens": tokens, "grad_out": grad_out, "w_in": w_in, "w_out": w_out, "rel_bias": rel_bias, "send_rows": send_rows, "recv_place": recv_place, "block_first": block_first, "user_rows": user_rows, "stamps": stamps}


EPS = 1e-05

def silu_slope(value):
    sigma = jax.nn.sigmoid(value)
    return sigma * (1.0 + value * (1.0 - sigma))

def owner_core(activated, own_g, first, live_rows, times, w_out, rel_bias):
    rows_dev = activated.shape[0]
    width = w_out.shape[0]
    head_dim = width // HEADS
    scale = head_dim ** (-0.5)
    row_first = jnp.repeat(first, BLOCK) * BLOCK
    row_live = jnp.repeat(live_rows, BLOCK)
    index = jnp.arange(rows_dev, dtype=jnp.int32)
    alive = index - row_first < row_live
    allowed = (row_first[:, None] == row_first[None, :]) & (index[None, :] <= index[:, None])
    allowed = allowed & alive[:, None] & alive[None, :]
    spread = times[:, None] - times[None, :]
    marks = jnp.left_shift(jnp.int32(1), jnp.arange(NBUCK - 1, dtype=jnp.int32))
    bucket = lax.optimization_barrier(jnp.sum((spread[:, :, None] >= marks[None, None, :]).astype(jnp.int32), axis=2))
    onehot = (bucket[:, :, None] == jnp.arange(NBUCK, dtype=jnp.int32)[None, None, :]).astype(jnp.float32)
    bias = jnp.einsum('ijb,hb->hij', onehot, rel_bias, precision=lax.Precision.HIGHEST)
    wide = activated.astype(jnp.float32)
    upper = wide[:, :width]
    values = wide[:, width:2 * width].reshape(rows_dev, HEADS, head_dim)
    queries = wide[:, 2 * width:3 * width].reshape(rows_dev, HEADS, head_dim)
    keys = wide[:, 3 * width:].reshape(rows_dev, HEADS, head_dim)
    logits = jnp.einsum('ihd,jhd->hij', queries, keys) * scale + bias
    weights = jnp.where(allowed[None], jax.nn.silu(logits), 0.0).astype(jnp.bfloat16)
    weights_f = weights.astype(jnp.float32)
    mixed = jnp.einsum('hij,jhd->ihd', weights_f, values).reshape(rows_dev, width)
    centre = mixed - lax.optimization_barrier(jnp.mean(mixed, axis=1, keepdims=True))
    inv_std = lax.rsqrt(lax.optimization_barrier(jnp.mean(centre * centre, axis=1, keepdims=True)) + EPS)
    normed = centre * inv_std
    gated = (normed * upper).astype(jnp.bfloat16)
    layer = lax.dot_general(gated, w_out, (((1,), (1,)), ((), ())), preferred_element_type=jnp.float32).astype(jnp.bfloat16)
    grad_gated = jnp.dot(own_g, w_out, preferred_element_type=jnp.float32)
    grad_upper = grad_gated * normed
    grad_normed = grad_gated * upper
    grad_mixed = inv_std * (grad_normed - lax.optimization_barrier(jnp.mean(grad_normed, axis=1, keepdims=True)) - normed * lax.optimization_barrier(jnp.mean(grad_normed * normed, axis=1, keepdims=True)))
    grad_mixed = grad_mixed.astype(jnp.bfloat16).astype(jnp.float32).reshape(rows_dev, HEADS, head_dim)
    grad_values = jnp.einsum('hij,ihd->jhd', weights_f, grad_mixed)
    grad_weights = jnp.einsum('ihd,jhd->hij', grad_mixed, values)
    grad_logits = jnp.where(allowed[None], grad_weights * silu_slope(logits), 0.0).astype(jnp.bfloat16).astype(jnp.float32)
    grad_queries = jnp.einsum('hij,jhd->ihd', grad_logits, keys) * scale
    grad_keys = jnp.einsum('hij,ihd->jhd', grad_logits, queries) * scale
    grad_act = jnp.concatenate([grad_upper, grad_values.reshape(rows_dev, width), grad_queries.reshape(rows_dev, width), grad_keys.reshape(rows_dev, width)], axis=1).astype(jnp.bfloat16)
    return (layer, gated, grad_act)

def reference(tokens, grad_out, w_in, w_out, rel_bias, send_rows, recv_place, block_first, user_rows, stamps):
    share = TOK_DEV // N_SEQ
    owner = jnp.arange(N_SEQ, dtype=jnp.int32)[:, None]
    loader = (recv_place // share).astype(jnp.int32)
    slot = (owner * share + recv_place % share).astype(jnp.int32)
    source = (loader * TOK_DEV + send_rows[loader, slot]).astype(jnp.int32)
    firsts = block_first.reshape(N_SEQ, BLOCKS_DEV)
    lives = user_rows.reshape(N_SEQ, BLOCKS_DEV)
    times = stamps.reshape(N_SEQ, TOK_DEV)

    def step(carry, item):
        rows_src, first, live, time_row = item
        own_x = tokens[rows_src]
        own_g = grad_out[rows_src]
        pre_act = jnp.dot(own_x, w_in, preferred_element_type=jnp.float32)
        activated = jax.nn.silu(pre_act).astype(jnp.bfloat16)
        layer, gated, grad_act = owner_core(activated, own_g, first, live, time_row, w_out, rel_bias)
        grad_pre = (grad_act.astype(jnp.float32) * silu_slope(pre_act)).astype(jnp.bfloat16)
        back = lax.dot_general(grad_pre, w_in, (((1,), (1,)), ((), ())), preferred_element_type=jnp.float32)
        grad_rows = (own_g.astype(jnp.float32) + back).astype(jnp.bfloat16)
        sum_in = carry[0] + lax.dot_general(own_x, grad_pre, (((0,), (0,)), ((), ())), preferred_element_type=jnp.float32)
        sum_out = carry[1] + lax.dot_general(own_g, gated, (((0,), (0,)), ((), ())), preferred_element_type=jnp.float32)
        out_rows = (own_x.astype(jnp.float32) + layer.astype(jnp.float32)).astype(jnp.bfloat16)
        return ((sum_in, sum_out), (out_rows, grad_rows))
    start = (jnp.zeros((D, 4 * D), jnp.float32), jnp.zeros((D, D), jnp.float32))
    sums, rows = lax.scan(step, start, (source, firsts, lives, times))
    flat = source.reshape(-1)
    out = jnp.zeros_like(tokens).at[flat].set(rows[0].reshape(-1, D))
    grad_x = jnp.zeros_like(tokens).at[flat].set(rows[1].reshape(-1, D))
    return (out, grad_x, sums[0], sums[1])
```

```python
import functools

import jax
import jax.numpy as jnp
from jax import lax
from jax.experimental import pallas as pl
from jax.experimental.pallas import tpu as pltpu
from jax.sharding import PartitionSpec as P

EPS = 1e-05
F32, BF16 = jnp.float32, jnp.bfloat16
MESH = pl.DeviceIdType.MESH
ORDERS = ((0, 0, 1, 2), (0, 1, 1, 2), (0, 1, 2, 2), (0, 0, 1, 2), (0, 1, 1, 2))
COUNT = tuple(sum(row.count(o) for row in ORDERS) for o in range(3))


def slots(block, order):
    start = sum(row.count(order) for row in ORDERS[:block])
    return start, ORDERS[block].count(order)


def dot(a, b, dims=((1,), (0,))):
    return lax.dot_general(a, b, (dims, ((), ())), preferred_element_type=F32)


def kernel(
    tok, gout, w_in, w_out, relb, srow, rplace, first, live, stamps,
    out, gx, gw1, gw2,
    wi, wo, sa, ra, sb, xg, meta, bias, mask, xv, gv, xt, gt, act, slp, pw, ps, mix, gg,
    stat, ga, gm, gp, b0, b1, b2, r10, r11, r12, s10, s11, s12, r20, r21, r22, s20, s21, s22,
    r30, r31, r32, fin, rfin, part, rpart, ret, ry, sz, rz,
    wsem, a_s, a_r, y_s, y_r, c_s, c_r, m_s, m_r, t_s, t_r, p1_s, p1_r, p2_s, p2_r, p3_s, p3_r,
    f_s, f_r, q_s, q_r, v_s, v_r, z_s, z_r,
):
    bs, r1, s1, r2 = (b0, b1, b2), (r10, r11, r12), (s10, s11, s12), (r20, r21, r22)
    s2, r3 = (s20, s21, s22), (r30, r31, r32)
    me = lax.axis_index("seq")
    c = lax.rem(me, 2)
    y = lax.rem(me // 2, 4)
    z = lax.rem(me // 8, 4)
    x = me // 32
    xz = me // 8
    low = lax.rem(me, 8)
    mate = me + 1 - 2 * c
    coords, strides = (x, z, y), (32, 8, 2)

    def along(axis, k):
        there = lax.rem(coords[axis] + k, 4)
        return there, me + (there - coords[axis]) * strides[axis]

    def rcopy(src, dst, send, recv, dev):
        return pltpu.make_async_remote_copy(
            src_ref=src, dst_ref=dst, send_sem=send, recv_sem=recv,
            device_id=(dev,), device_id_type=MESH,
        )

    barrier = pltpu.get_barrier_semaphore()

    @pl.loop(1, 16)
    def _(k):
        pl.semaphore_signal(
            barrier, inc=1, device_id=(lax.rem(xz + k, 16) * 8 + low,), device_id_type=MESH
        )

    for k in range(1, 4):
        pl.semaphore_signal(barrier, inc=1, device_id=(along(2, k)[1],), device_id_type=MESH)
    pl.semaphore_signal(barrier, inc=1, device_id=(mate,), device_id_type=MESH)

    half = pl.multiple_of(c * 512, 512)
    loads = [
        pltpu.make_async_copy(w_in.at[:, pl.ds(f * 1024 + half, 512)], wi.at[f], wsem.at[f])
        for f in range(4)
    ]
    loads.append(pltpu.make_async_copy(w_out.at[:, pl.ds(half, 512)], wo, wsem.at[4]))
    for load in loads:
        load.start()

    rows = lax.broadcasted_iota(jnp.int32, (128, 128), 0)
    lanes = lax.broadcasted_iota(jnp.int32, (128, 128), 1)
    eye = rows == lanes

    def to_column(row):
        return jnp.sum(jnp.where(eye, row, 0.0), axis=1, keepdims=True)

    def to_row(column):
        return jnp.sum(jnp.where(eye, column, 0.0), axis=0, keepdims=True)

    wanted = to_column(srow[...].astype(F32))
    pick = jnp.where(wanted == lanes.astype(F32), 1.0, 0.0).astype(BF16)
    sent = jnp.concatenate(
        [dot(pick, tok[...]).reshape(16, 8, 1024), dot(pick, gout[...]).reshape(16, 8, 1024)],
        axis=1,
    )
    sa[...] = sent.astype(BF16)

    pl.semaphore_wait(barrier, 19)

    @pl.loop(1, 16)
    def _(k):
        to = lax.rem(xz + k, 16)
        rcopy(sa.at[to], ra.at[xz], a_s.at[k], a_r.at[k], to * 8 + low).start()

    ra[xz] = sa[xz]

    m = rplace[...]
    place = (m & 1) * 64 + ((m >> 1) & 3) * 16 + (m >> 5) * 4 + ((m >> 3) & 3)
    lands = place == rows
    slot = to_row(jnp.sum(jnp.where(lands, lanes.astype(F32), 0.0), axis=1, keepdims=True))
    when = to_row(jnp.sum(jnp.where(lands, stamps[...].astype(F32), 0.0), axis=1, keepdims=True))
    alive = slot < (live[0] + first[0] * 128).astype(F32)
    sub = lax.broadcasted_iota(jnp.int32, (8, 128), 0)
    meta[c] = jnp.where(
        sub == 0,
        jnp.where(alive, slot, 1e6),
        jnp.where(sub == 1, jnp.where(alive, slot, -1.0), when),
    )
    meta_copy = rcopy(meta.at[c], meta.at[c], m_s, m_r, mate)
    meta_copy.start()

    def wait_meta():
        rcopy(meta.at[1 - c], meta.at[1 - c], m_s, m_r, mate).wait_recv()

    wait_meta()
    for o in range(2):
        keys, asks, times = meta[o, 0:1], to_column(meta[o, 1:2]), meta[o, 2:3]
        mask[o] = jnp.where(keys <= asks, 1.0, 0.0)
        spread = to_column(times) - times

        @pl.loop(0, 4)
        def _(h, o=o, spread=spread):
            value = jnp.full((128, 128), relb[4 * c + h, 0], F32)
            for k in range(15):
                value = jnp.where(spread >= float(2**k), relb[4 * c + h, k + 1], value)
            bias[4 * o + h] = value

    @pl.loop(1, 16)
    def _(k):
        come = lax.rem(xz + 16 - k, 16)
        rcopy(sa.at[come], ra.at[come], a_s.at[k], a_r.at[k], come * 8 + low).wait_recv()

    r256 = lax.broadcasted_iota(jnp.int32, (256, 256), 0)
    l256 = lax.broadcasted_iota(jnp.int32, (256, 256), 1)

    def swapped(r):
        return (r & 15) * 16 + ((r >> 5) & 1) * 8 + (r >> 6) * 2 + ((r >> 4) & 1)

    turn = jnp.where(l256 == swapped(r256), 1.0, 0.0).astype(BF16)
    sb[...] = dot(turn, ra[...].reshape(256, 1024)).astype(BF16).reshape(4, 2, 2, 16, 1024)
    for k in range(1, 4):
        to, dev = along(2, k)
        rcopy(sb.at[to], xg.at[c, y], y_s.at[k], y_r.at[k], dev).start()
    xg[c, y] = sb[y]
    rcopy(xg.at[c, y], xg.at[c, y], c_s.at[0], c_r.at[0], mate).start()
    for k in range(1, 4):
        come = lax.rem(y + 4 - k, 4)
        rcopy(sb.at[come], xg.at[c, come], y_s.at[k], y_r.at[k], me).wait_recv()
        rcopy(xg.at[c, come], xg.at[c, come], c_s.at[k], c_r.at[k], mate).start()
    for k in range(4):
        come = lax.rem(y + 4 - k, 4)
        rcopy(xg.at[1 - c, come], xg.at[1 - c, come], c_s.at[k], c_r.at[k], mate).wait_recv()

    for o in range(2):
        xv[128 * o : 128 * o + 128] = xg[:, :, 0, o].reshape(128, 1024)
        gv[128 * o : 128 * o + 128] = xg[:, :, 1, o].reshape(128, 1024)

    for load in loads:
        load.wait()

    for f in range(4):
        pre = dot(xv[...], wi[f])
        sig = jax.nn.sigmoid(pre)
        act[f] = (pre * sig).astype(BF16)
        slp[f] = sig * (1.0 + pre * (1.0 - sig))
    gg[...] = dot(gv[...], wo[...])
    heads = [(o, h) for o in range(2) for h in range(4)]
    scale = 128**-0.5
    for o, h in heads:
        here = (slice(128 * o, 128 * o + 128), slice(128 * h, 128 * h + 128))
        v, q, k = (act[(f,) + here] for f in (1, 2, 3))
        logits = dot(q, k, ((1,), (1,))) * scale + bias[4 * o + h]
        sig = jax.nn.sigmoid(logits)
        allowed = mask[o] > 0.5
        w = jnp.where(allowed, logits * sig, 0.0).astype(BF16)
        pw[4 * o + h] = w
        ps[4 * o + h] = jnp.where(allowed, sig * (1.0 + logits * (1.0 - sig)), 0.0)
        mix[here] = dot(w, v)

    gn = gg[...] * act[0].astype(F32)
    mixed = mix[...]
    total = jnp.sum(mixed, axis=1, keepdims=True)
    centre = mixed - total * (1.0 / 512)
    square = jnp.sum(centre * centre, axis=1, keepdims=True)
    gsum = jnp.sum(gn, axis=1, keepdims=True)
    gdot = jnp.sum(gn * centre, axis=1, keepdims=True)
    col = lax.broadcasted_iota(jnp.int32, (256, 128), 1)
    stat[c] = jnp.where(
        col == 0, total, jnp.where(col == 1, square, jnp.where(col == 2, gsum, gdot))
    )
    stat_copy = rcopy(stat.at[c], stat.at[c], t_s, t_r, mate)
    stat_copy.start()
    xt[...] = xv[...].T
    gt[...] = gv[...].T
    rcopy(stat.at[1 - c], stat.at[1 - c], t_s, t_r, mate).wait_recv()
    theirs = stat[1 - c]
    total2, square2, gsum2, gdot2 = (theirs[:, i : i + 1] for i in range(4))
    mean = (total + total2) * (1.0 / 1024)
    off, off2 = total * (1.0 / 512) - mean, total2 * (1.0 / 512) - mean
    var = (square + square2 + 512.0 * (off * off + off2 * off2)) * (1.0 / 1024)
    inv_std = lax.rsqrt(var + EPS)
    mean_gn = (gsum + gsum2) * (1.0 / 1024)
    mean_gnn = (gdot + off * gsum + gdot2 + off2 * gsum2) * inv_std * (1.0 / 1024)
    normed = (mix[...] - mean) * inv_std
    upper = act[0].astype(F32)
    ga[...] = (normed * upper).astype(BF16)
    ggv = gg[...]
    gm[...] = (inv_std * (ggv * upper - mean_gn - normed * mean_gnn)).astype(BF16)
    gp[0] = ((ggv * normed).astype(BF16).astype(F32) * slp[0]).astype(BF16)

    def product(block, left, right):
        @pl.loop(0, 4)
        def _(i):
            rows = pl.ds(pl.multiple_of(i * 256, 256), 256)
            tile = dot(left[rows, :], right).astype(BF16)
            seen = [0, 0, 0]
            for j in range(4):
                o = ORDERS[block][j]
                at = slots(block, o)[0] + seen[o]
                seen[o] += 1
                part4 = tile[:, 128 * j : 128 * j + 128].reshape(4, 4, 16, 128)
                if o == 0:
                    bs[0][at, i] = part4
                elif o == 1:
                    bs[1][at, :, :, i] = part4
                else:
                    for k in range(4):
                        bs[2][at, :, i, k] = part4[k]

    def hop(stage, block, o, k):
        axis = (o + stage) % 3
        there, dev = along(axis, k)
        if stage < 2:
            start, count = slots(block, o)
            at = pl.ds(start, count)
            i = (block * 3 + o) * 3 + k - 1
            src, dst = ((bs, r1), (s1, r2))[stage]
            send, recv = ((p1_s, p1_r), (p2_s, p2_r))[stage]
            return rcopy(
                src[o].at[at, there], dst[o].at[k - 1, at], send.at[i], recv.at[i], dev
            )
        i = o * 3 + k - 1
        return rcopy(s2[o].at[:, there], r3[o].at[k - 1], p3_s.at[i], p3_r.at[i], dev)

    def send(stage, block):
        for k in (2, 1, 3):
            for o in range(3):
                hop(stage, block, o, k).start()

    def add(stage, block):
        for o in range(3):
            for k in range(1, 4):
                hop(stage, block, o, k).wait_recv()
            here = coords[(o + stage) % 3]
            start, count = slots(block, o)
            at = slice(start, start + count)
            if stage == 0:
                value = bs[o][at, here].astype(F32)
                for k in range(3):
                    value = value + r1[o][k, at].astype(F32)
                s1[o][at] = value.astype(BF16)
            else:
                value = s1[o][at, here].astype(F32)
                for k in range(3):
                    value = value + r2[o][k, at].astype(F32)
                s2[o][at] = value.astype(BF16)

    product(0, gt, ga[...])
    send(0, 0)
    product(1, xt, gp[0])
    send(0, 1)
    part[0] = dot(ga[...], wo[...], ((1,), (1,))).reshape(2, 2, 64, 1024)

    for o, h in heads:
        here = (slice(128 * o, 128 * o + 128), slice(128 * h, 128 * h + 128))
        v, q, k = (act[(f,) + here] for f in (1, 2, 3))
        gmh, w = gm[here], pw[4 * o + h]
        gl = (dot(gmh, v, ((1,), (1,))) * ps[4 * o + h]).astype(BF16)
        grads = (
            dot(w, gmh, ((0,), (0,))),
            dot(gl, k) * scale,
            dot(gl, q, ((0,), (0,))) * scale,
        )
        for f in (1, 2, 3):
            gp[(f,) + here] = (
                grads[f - 1].astype(BF16).astype(F32) * slp[(f,) + here]
            ).astype(BF16)

    product(2, xt, gp[1])
    send(0, 2)
    product(3, xt, gp[2])
    send(0, 3)
    product(4, xt, gp[3])
    send(0, 4)
    back = dot(gp[0], wi[0], ((1,), (1,)))
    for f in range(1, 4):
        back = back + dot(gp[f], wi[f], ((1,), (1,)))
    part[1] = back.reshape(2, 2, 64, 1024)
    core = rcopy(part.at[:, :, 1 - c], rpart, q_s, q_r, mate)
    core.start()
    core.wait_recv()
    for o in range(2):
        layer = (part[0, o, c] + rpart[0, o]).astype(BF16)
        grad = xg[c, :, 1, o].astype(F32) + (part[1, o, c] + rpart[1, o]).reshape(4, 16, 1024)
        ret[:, 0, o] = layer.reshape(4, 16, 1024)
        ret[:, 1, o] = grad.astype(BF16)
    for k in range(1, 4):
        to, dev = along(2, k)
        rcopy(ret.at[to], ry.at[y], v_s.at[k], v_r.at[k], dev).start()
    ry[y] = ret[y]
    add(0, 0)
    send(1, 0)
    for k in range(1, 4):
        come = lax.rem(y + 4 - k, 4)
        rcopy(ret.at[come], ry.at[come], v_s.at[k], v_r.at[k], me).wait_recv()
    unturn = jnp.where(r256 == swapped(l256), 1.0, 0.0).astype(BF16)
    sz[...] = dot(unturn, ry[...].reshape(256, 1024)).astype(BF16).reshape(16, 16, 1024)

    @pl.loop(1, 16)
    def _(k):
        to = lax.rem(xz + k, 16)
        rcopy(sz.at[to], rz.at[xz], z_s.at[k], z_r.at[k], to * 8 + low).start()

    rz[xz] = sz[xz]
    for block in range(1, 5):
        add(0, block)
        send(1, block)

    @pl.loop(1, 16)
    def _(k):
        come = lax.rem(xz + 16 - k, 16)
        rcopy(sz.at[come], rz.at[come], z_s.at[k], z_r.at[k], come * 8 + low).wait_recv()

    got = rz[...].astype(F32)
    unpick = jnp.where(srow[...] == rows, 1.0, 0.0).astype(BF16)
    layer = dot(unpick, got[:, :8].reshape(128, 1024).astype(BF16))
    out[...] = (tok[...].astype(F32) + layer).astype(BF16)
    gx[...] = dot(unpick, got[:, 8:].reshape(128, 1024).astype(BF16)).astype(BF16)

    for block in range(5):
        add(1, block)
    for k in (2, 1, 3):
        for o in range(3):
            hop(2, 0, o, k).start()
    for o in range(3):
        for k in range(1, 4):
            hop(2, 0, o, k).wait_recv()
        value = s2[o][:, coords[(o + 2) % 3]].astype(F32)
        for k in range(3):
            value = value + r3[o][k].astype(F32)
        for block in range(5):
            start, _ = slots(block, o)
            mine = [j for j in range(4) if ORDERS[block][j] == o]
            for n, j in enumerate(mine):
                fin[4 * block + j] = value[start + n]
    away, home = pl.multiple_of(8 * (1 - c), 8), pl.multiple_of(8 * c, 8)
    last = rcopy(fin.at[:, pl.ds(away, 8)], rfin, f_s, f_r, mate)
    last.start()
    other = pl.multiple_of(512 - half, 512)
    mine = fin[:, pl.ds(home, 8)]
    for j in range(4):
        gw2[:, pl.ds(half + 128 * j, 128)] = mine[j]
        for f in range(4):
            gw1[:, pl.ds(f * 1024 + half + 128 * j, 128)] = mine[4 + 4 * f + j]
    last.wait_recv()
    for j in range(4):
        gw2[:, pl.ds(other + 128 * j, 128)] = rfin[j]
        for f in range(4):
            gw1[:, pl.ds(f * 1024 + other + 128 * j, 128)] = rfin[4 + 4 * f + j]

    @pl.loop(1, 16)
    def _(k):
        to = lax.rem(xz + k, 16)
        rcopy(sa.at[to], ra.at[xz], a_s.at[k], a_r.at[k], to * 8 + low).wait_send()
        rcopy(sz.at[to], rz.at[xz], z_s.at[k], z_r.at[k], to * 8 + low).wait_send()

    meta_copy.wait_send()
    stat_copy.wait_send()
    core.wait_send()
    last.wait_send()
    for k in range(4):
        come = lax.rem(y + 4 - k, 4)
        rcopy(xg.at[c, come], xg.at[c, come], c_s.at[k], c_r.at[k], mate).wait_send()
    for k in range(1, 4):
        to, dev = along(2, k)
        rcopy(sb.at[to], xg.at[c, y], y_s.at[k], y_r.at[k], dev).wait_send()
        rcopy(ret.at[to], ry.at[y], v_s.at[k], v_r.at[k], dev).wait_send()
        for o in range(3):
            for block in range(5):
                hop(0, block, o, k).wait_send()
                hop(1, block, o, k).wait_send()
            hop(2, 0, o, k).wait_send()


def body(
    tokens, grad_out, w_in, w_out, rel_bias, send_rows, recv_place, block_first, user_rows, stamps
):
    vmem, smem = pl.BlockSpec(memory_space=pltpu.VMEM), pl.BlockSpec(memory_space=pltpu.SMEM)
    hbm = pl.BlockSpec(memory_space=pl.ANY)
    dma = pltpu.SemaphoreType.DMA

    def v(shape, kind=BF16):
        return pltpu.VMEM(shape, kind)

    scratch = [
        v((4, 1024, 512)), v((1024, 512)), v((16, 16, 1024)), v((16, 16, 1024)),
        v((4, 2, 2, 16, 1024)), v((2, 4, 2, 2, 16, 1024)), v((2, 8, 128), F32),
        v((8, 128, 128), F32), v((2, 128, 128), F32), v((256, 1024)), v((256, 1024)),
        v((1024, 256)), v((1024, 256)), v((4, 256, 512)), v((4, 256, 512), F32),
        v((8, 128, 128)), v((8, 128, 128), F32), v((256, 512), F32), v((256, 512), F32),
        v((2, 256, 128), F32), v((256, 512)), v((256, 512)), v((4, 256, 512)),
    ]
    scratch += [v((n, 4, 4, 4, 16, 128)) for n in COUNT]
    scratch += [v((3, n, 4, 4, 16, 128)) for n in COUNT]
    scratch += [v((n, 4, 4, 16, 128)) for n in COUNT]
    scratch += [v((3, n, 4, 16, 128)) for n in COUNT]
    scratch += [v((n, 4, 16, 128)) for n in COUNT]
    scratch += [v((3, n, 16, 128)) for n in COUNT]
    scratch += [
        v((20, 16, 128), F32), v((20, 8, 128), F32), v((2, 2, 2, 64, 1024), F32),
        v((2, 2, 64, 1024), F32), v((4, 2, 2, 16, 1024)), v((4, 2, 2, 16, 1024)),
        v((16, 16, 1024)), v((16, 16, 1024)),
    ]
    scratch += [dma((5,)), dma((16,)), dma((16,)), dma((4,)), dma((4,)), dma((4,)), dma((4,))]
    scratch += [dma, dma, dma, dma, dma((45,)), dma((45,)), dma((45,)), dma((45,))]
    scratch += [dma((9,)), dma((9,)), dma, dma, dma, dma, dma((4,)), dma((4,)), dma((16,)), dma((16,))]
    return tuple(
        pl.pallas_call(
            kernel,
            out_shape=(
                jax.ShapeDtypeStruct((128, 1024), BF16),
                jax.ShapeDtypeStruct((128, 1024), BF16),
                jax.ShapeDtypeStruct((8, 4096), F32),
                jax.ShapeDtypeStruct((8, 1024), F32),
            ),
            in_specs=[vmem, vmem, hbm, hbm, smem, vmem, vmem, smem, smem, vmem],
            out_specs=(vmem, vmem, vmem, vmem),
            scratch_shapes=scratch,
            compiler_params=pltpu.CompilerParams(
                collective_id=0, has_side_effects=True, vmem_limit_bytes=56 * 2**20
            ),
        )(
            tokens, grad_out, w_in, w_out, rel_bias, send_rows, recv_place, block_first,
            user_rows, stamps.reshape(1, 128),
        )
    )


def solution(mesh):
    placed = (
        P("seq", None), P("seq", None), P(), P(), P(), P("seq", None), P("seq", None),
        P("seq"), P("seq"), P("seq"),
    )
    return jax.shard_map(
        body,
        mesh=mesh,
        in_specs=placed,
        out_specs=(P("seq", None), P("seq", None), P("seq", None), P("seq", None)),
        check_vma=False,
    )
```

```python
import functools

import jax
import jax.numpy as jnp
from jax import lax
from jax.experimental import pallas as pl
from jax.experimental.pallas import tpu as pltpu
from jax.sharding import PartitionSpec as P

EPS = 1e-05
F32, BF16 = jnp.float32, jnp.bfloat16
MESH = pl.DeviceIdType.MESH
ORDERS = ((0, 0, 1, 2), (0, 1, 1, 2), (0, 1, 2, 2), (0, 0, 1, 2), (0, 1, 1, 2))
COUNT = tuple(sum(row.count(o) for row in ORDERS) for o in range(3))


def slots(block, order):
    start = sum(row.count(order) for row in ORDERS[:block])
    return start, ORDERS[block].count(order)


def dot(a, b, dims=((1,), (0,))):
    return lax.dot_general(a, b, (dims, ((), ())), preferred_element_type=F32)


def kernel(
    tok, gout, w_in, w_out, relb, srow, rplace, first, live, stamps,
    out, gx, gw1, gw2,
    wi, wo, sf, sa, rg, rf, meta, bias, mask, xv, gv, xt, gt, act, slp, pw, ps, mix, gg,
    stat, ga, gm, gp, b0, b1, b2, r10, r11, r12, s10, s11, s12, r20, r21, r22, s20, s21, s22,
    r30, r31, r32, fin, rfin, part, rpart, rz,
    wsem, a_s, a_r, c_s, c_r, m_s, m_r, t_s, t_r, p1_s, p1_r, p2_s, p2_r, p3_s, p3_r,
    f_s, f_r, q_s, q_r, z_s, z_r,
):
    bs, r1, s1, r2 = (b0, b1, b2), (r10, r11, r12), (s10, s11, s12), (r20, r21, r22)
    s2, r3 = (s20, s21, s22), (r30, r31, r32)
    me = lax.axis_index("seq")
    c = lax.rem(me, 2)
    y = lax.rem(me // 2, 4)
    z = lax.rem(me // 8, 4)
    x = me // 32
    chip = me // 2
    mate = me + 1 - 2 * c
    coords, strides = (x, z, y), (32, 8, 2)

    def along(axis, k):
        there = lax.rem(coords[axis] + k, 4)
        return there, me + (there - coords[axis]) * strides[axis]

    def rcopy(src, dst, send, recv, dev):
        return pltpu.make_async_remote_copy(
            src_ref=src, dst_ref=dst, send_sem=send, recv_sem=recv,
            device_id=(dev,), device_id_type=MESH,
        )

    barrier = pltpu.get_barrier_semaphore()

    @pl.loop(1, 64)
    def _(k):
        pl.semaphore_signal(
            barrier, inc=1, device_id=(lax.rem(chip + k, 64) * 2 + c,), device_id_type=MESH
        )

    pl.semaphore_signal(barrier, inc=1, device_id=(mate,), device_id_type=MESH)

    half = pl.multiple_of(c * 512, 512)
    loads = [
        pltpu.make_async_copy(w_in.at[:, pl.ds(f * 1024 + half, 512)], wi.at[f], wsem.at[f])
        for f in range(4)
    ]
    loads.append(pltpu.make_async_copy(w_out.at[:, pl.ds(half, 512)], wo, wsem.at[4]))
    for load in loads:
        load.start()

    rows = lax.broadcasted_iota(jnp.int32, (128, 128), 0)
    lanes = lax.broadcasted_iota(jnp.int32, (128, 128), 1)
    eye = rows == lanes

    def to_column(row):
        return jnp.sum(jnp.where(eye, row, 0.0), axis=1, keepdims=True)

    def to_row(column):
        return jnp.sum(jnp.where(eye, column, 0.0), axis=0, keepdims=True)

    order = ((rows & 63) << 1) + (rows >> 6)
    wanted = jnp.sum(
        jnp.where(lanes == order, srow[...].astype(F32), 0.0), axis=1, keepdims=True
    )
    pick = jnp.where(wanted == lanes.astype(F32), 1.0, 0.0).astype(BF16)

    def fold(value, kind):
        for o in range(2):
            for j in range(8):
                sf[pl.ds(kind * 16 + o * 8 + j, 64, stride=32), :] = value[
                    64 * o : 64 * o + 64, 128 * j : 128 * j + 128
                ]

    def unfolded(ref, kind, o):
        return jnp.concatenate(
            [ref[pl.ds(kind * 16 + o * 8 + j, 64, stride=32), :] for j in range(8)], axis=1
        )

    fold(dot(pick, tok[...]), 0)
    fold(dot(pick, gout[...]), 1)
    sa[...] = sf[...].reshape(64, 32, 128).astype(BF16)

    pl.semaphore_wait(barrier, 64)

    def peer(i, j):
        there = lax.rem(x + i, 4) * 16 + lax.rem(z * 4 + y + j, 16)
        return there, there * 2 + c

    def scatter(src, dst, sends, recvs):
        @pl.loop(0, 16)
        def _(j):
            for i in range(4):
                there, dev = peer(i, j)

                def go():
                    rcopy(src.at[there], dst.at[chip], sends.at[i], recvs.at[i], dev).start()

                if i == 0:
                    pl.when(j > 0)(go)
                else:
                    go()

    def scattered(src, dst, sends, recvs, i):
        come = lax.rem(x + 4 - i, 4) * 16
        at = pl.ds(come, 16 if i else 15)
        return rcopy(src.at[at], dst.at[at], sends.at[i], recvs.at[i], mate)

    scatter(sa, rg.at[c], a_s, a_r)
    rg[c, chip] = sa[chip]

    m = rplace[...]
    place = (m & 1) * 64 + (m >> 1)
    lands = place == rows
    slot = to_row(jnp.sum(jnp.where(lands, lanes.astype(F32), 0.0), axis=1, keepdims=True))
    when = to_row(jnp.sum(jnp.where(lands, stamps[...].astype(F32), 0.0), axis=1, keepdims=True))
    alive = slot < (live[0] + first[0] * 128).astype(F32)
    sub = lax.broadcasted_iota(jnp.int32, (8, 128), 0)
    meta[c] = jnp.where(
        sub == 0,
        jnp.where(alive, slot, 1e6),
        jnp.where(sub == 1, jnp.where(alive, slot, -1.0), when),
    )
    meta_copy = rcopy(meta.at[c], meta.at[c], m_s, m_r, mate)
    meta_copy.start()

    def wait_meta():
        rcopy(meta.at[1 - c], meta.at[1 - c], m_s, m_r, mate).wait_recv()

    wait_meta()
    for o in range(2):
        keys, asks, times = meta[o, 0:1], to_column(meta[o, 1:2]), meta[o, 2:3]
        mask[o] = jnp.where(keys <= asks, 1.0, 0.0)
        spread = to_column(times) - times

        @pl.loop(0, 4)
        def _(h, o=o, spread=spread):
            value = jnp.full((128, 128), relb[4 * c + h, 0], F32)
            for k in range(15):
                value = jnp.where(spread >= float(2**k), relb[4 * c + h, k + 1], value)
            bias[4 * o + h] = value

    def forward(cs, i):
        at = pl.ds(lax.rem(x + 4 - i, 4) * 16, 16)
        return rcopy(rg.at[cs, at], rg.at[cs, at], c_s.at[i], c_r.at[i], mate)

    def widen(cs, i):
        at = lax.rem(x + 4 - i, 4)
        wide = rg[cs, pl.ds(at * 16, 16)].astype(F32).reshape(512, 128)
        rf[cs, pl.ds(pl.multiple_of(at * 512, 512), 512)] = wide

    for i in (0, 1, 3, 2):
        scattered(sa, rg.at[c], a_s, a_r, i).wait_recv()
        forward(c, i).start()
        widen(c, i)
    for i in (0, 1, 3, 2):
        forward(1 - c, i).wait_recv()
        widen(1 - c, i)
        scattered(sa, rg.at[c], a_s, a_r, i).wait_send()
    for o in range(2):
        for cs in range(2):
            here = slice(128 * o + 64 * cs, 128 * o + 64 * cs + 64)
            xv[here] = unfolded(rf.at[cs], 0, o).astype(BF16)
            gv[here] = unfolded(rf.at[cs], 1, o).astype(BF16)

    for load in loads:
        load.wait()

    for f in range(4):
        pre = dot(xv[...], wi[f])
        sig = jax.nn.sigmoid(pre)
        act[f] = (pre * sig).astype(BF16)
        slp[f] = sig * (1.0 + pre * (1.0 - sig))
    gg[...] = dot(gv[...], wo[...])
    heads = [(o, h) for o in range(2) for h in range(4)]
    scale = 128**-0.5
    for o, h in heads:
        here = (slice(128 * o, 128 * o + 128), slice(128 * h, 128 * h + 128))
        v, q, k = (act[(f,) + here] for f in (1, 2, 3))
        logits = dot(q, k, ((1,), (1,))) * scale + bias[4 * o + h]
        sig = jax.nn.sigmoid(logits)
        allowed = mask[o] > 0.5
        w = jnp.where(allowed, logits * sig, 0.0).astype(BF16)
        pw[4 * o + h] = w
        ps[4 * o + h] = jnp.where(allowed, sig * (1.0 + logits * (1.0 - sig)), 0.0)
        mix[here] = dot(w, v)

    gn = gg[...] * act[0].astype(F32)
    mixed = mix[...]
    total = jnp.sum(mixed, axis=1, keepdims=True)
    centre = mixed - total * (1.0 / 512)
    square = jnp.sum(centre * centre, axis=1, keepdims=True)
    gsum = jnp.sum(gn, axis=1, keepdims=True)
    gdot = jnp.sum(gn * centre, axis=1, keepdims=True)
    col = lax.broadcasted_iota(jnp.int32, (256, 128), 1)
    stat[c] = jnp.where(
        col == 0, total, jnp.where(col == 1, square, jnp.where(col == 2, gsum, gdot))
    )
    stat_copy = rcopy(stat.at[c], stat.at[c], t_s, t_r, mate)
    stat_copy.start()
    xt[...] = xv[...].T
    gt[...] = gv[...].T
    rcopy(stat.at[1 - c], stat.at[1 - c], t_s, t_r, mate).wait_recv()
    theirs = stat[1 - c]
    total2, square2, gsum2, gdot2 = (theirs[:, i : i + 1] for i in range(4))
    mean = (total + total2) * (1.0 / 1024)
    off, off2 = total * (1.0 / 512) - mean, total2 * (1.0 / 512) - mean
    var = (square + square2 + 512.0 * (off * off + off2 * off2)) * (1.0 / 1024)
    inv_std = lax.rsqrt(var + EPS)
    mean_gn = (gsum + gsum2) * (1.0 / 1024)
    mean_gnn = (gdot + off * gsum + gdot2 + off2 * gsum2) * inv_std * (1.0 / 1024)
    normed = (mix[...] - mean) * inv_std
    upper = act[0].astype(F32)
    ga[...] = (normed * upper).astype(BF16)
    ggv = gg[...]
    gm[...] = (inv_std * (ggv * upper - mean_gn - normed * mean_gnn)).astype(BF16)
    gp[0] = ((ggv * normed).astype(BF16).astype(F32) * slp[0]).astype(BF16)

    def product(block, left, right):
        @pl.loop(0, 4)
        def _(i):
            rows = pl.ds(pl.multiple_of(i * 256, 256), 256)
            tile = dot(left[rows, :], right).astype(BF16)
            seen = [0, 0, 0]
            for j in range(4):
                o = ORDERS[block][j]
                at = slots(block, o)[0] + seen[o]
                seen[o] += 1
                part4 = tile[:, 128 * j : 128 * j + 128].reshape(4, 4, 16, 128)
                if o == 0:
                    bs[0][at, i] = part4
                elif o == 1:
                    bs[1][at, :, :, i] = part4
                else:
                    for k in range(4):
                        bs[2][at, :, i, k] = part4[k]

    def hop(stage, block, o, k):
        axis = (o + stage) % 3
        there, dev = along(axis, k)
        if stage < 2:
            start, count = slots(block, o)
            at = pl.ds(start, count)
            i = (block * 3 + o) * 3 + k - 1
            src, dst = ((bs, r1), (s1, r2))[stage]
            send, recv = ((p1_s, p1_r), (p2_s, p2_r))[stage]
            return rcopy(
                src[o].at[at, there], dst[o].at[k - 1, at], send.at[i], recv.at[i], dev
            )
        i = o * 3 + k - 1
        return rcopy(s2[o].at[:, there], r3[o].at[k - 1], p3_s.at[i], p3_r.at[i], dev)

    def send(stage, block):
        for k in (2, 1, 3):
            for o in range(3):
                hop(stage, block, o, k).start()

    def add(stage, block):
        for o in range(3):
            for k in range(1, 4):
                hop(stage, block, o, k).wait_recv()
            here = coords[(o + stage) % 3]
            start, count = slots(block, o)
            at = slice(start, start + count)
            if stage == 0:
                value = bs[o][at, here].astype(F32)
                for k in range(3):
                    value = value + r1[o][k, at].astype(F32)
                s1[o][at] = value.astype(BF16)
            else:
                value = s1[o][at, here].astype(F32)
                for k in range(3):
                    value = value + r2[o][k, at].astype(F32)
                s2[o][at] = value.astype(BF16)

    product(0, gt, ga[...])
    send(0, 0)
    product(1, xt, gp[0])
    send(0, 1)
    part[0] = dot(ga[...], wo[...], ((1,), (1,))).reshape(2, 2, 64, 1024)

    for o, h in heads:
        here = (slice(128 * o, 128 * o + 128), slice(128 * h, 128 * h + 128))
        v, q, k = (act[(f,) + here] for f in (1, 2, 3))
        gmh, w = gm[here], pw[4 * o + h]
        gl = (dot(gmh, v, ((1,), (1,))) * ps[4 * o + h]).astype(BF16)
        grads = (
            dot(w, gmh, ((0,), (0,))),
            dot(gl, k) * scale,
            dot(gl, q, ((0,), (0,))) * scale,
        )
        for f in (1, 2, 3):
            gp[(f,) + here] = (
                grads[f - 1].astype(BF16).astype(F32) * slp[(f,) + here]
            ).astype(BF16)

    product(2, xt, gp[1])
    send(0, 2)
    product(3, xt, gp[2])
    send(0, 3)
    product(4, xt, gp[3])
    send(0, 4)
    back = dot(gp[0], wi[0], ((1,), (1,)))
    for f in range(1, 4):
        back = back + dot(gp[f], wi[f], ((1,), (1,)))
    part[1] = back.reshape(2, 2, 64, 1024)
    core = rcopy(part.at[:, :, 1 - c], rpart, q_s, q_r, mate)
    core.start()
    core.wait_recv()
    mine = pl.multiple_of(64 * c, 64)
    for o in range(2):
        layer, grad = (part[i, o, c] + rpart[i, o] for i in range(2))
        for j in range(8):
            cols = slice(128 * j, 128 * j + 128)
            own = gv[pl.ds(128 * o + mine, 64), cols].astype(F32)
            sf[pl.ds(o * 8 + j, 64, stride=32), :] = layer[:, cols]
            sf[pl.ds(16 + o * 8 + j, 64, stride=32), :] = own + grad[:, cols]
    sa[...] = sf[...].reshape(64, 32, 128).astype(BF16)
    scatter(sa, rz, z_s, z_r)
    rz[chip] = sa[chip]
    add(0, 0)
    send(1, 0)
    for block in range(1, 5):
        add(0, block)
        send(1, block)

    for i in range(4):
        scattered(sa, rz, z_s, z_r, i).wait_recv()
    sf[...] = rz[...].astype(F32).reshape(2048, 128)
    unpick = jnp.where(to_row(wanted) == rows.astype(F32), 1.0, 0.0).astype(BF16)
    layer, grad = (
        dot(unpick, jnp.concatenate([unfolded(sf, i, 0), unfolded(sf, i, 1)], axis=0).astype(BF16))
        for i in range(2)
    )
    out[...] = (tok[...].astype(F32) + layer).astype(BF16)
    gx[...] = grad.astype(BF16)

    for block in range(5):
        add(1, block)
    for k in (2, 1, 3):
        for o in range(3):
            hop(2, 0, o, k).start()
    for o in range(3):
        for k in range(1, 4):
            hop(2, 0, o, k).wait_recv()
        value = s2[o][:, coords[(o + 2) % 3]].astype(F32)
        for k in range(3):
            value = value + r3[o][k].astype(F32)
        for block in range(5):
            start, _ = slots(block, o)
            mine = [j for j in range(4) if ORDERS[block][j] == o]
            for n, j in enumerate(mine):
                fin[4 * block + j] = value[start + n]
    away, home = pl.multiple_of(8 * (1 - c), 8), pl.multiple_of(8 * c, 8)
    last = rcopy(fin.at[:, pl.ds(away, 8)], rfin, f_s, f_r, mate)
    last.start()
    other = pl.multiple_of(512 - half, 512)
    mine = fin[:, pl.ds(home, 8)]
    for j in range(4):
        gw2[:, pl.ds(half + 128 * j, 128)] = mine[j]
        for f in range(4):
            gw1[:, pl.ds(f * 1024 + half + 128 * j, 128)] = mine[4 + 4 * f + j]
    last.wait_recv()
    for j in range(4):
        gw2[:, pl.ds(other + 128 * j, 128)] = rfin[j]
        for f in range(4):
            gw1[:, pl.ds(f * 1024 + other + 128 * j, 128)] = rfin[4 + 4 * f + j]

    for i in range(4):
        scattered(sa, rz, z_s, z_r, i).wait_send()

    meta_copy.wait_send()
    stat_copy.wait_send()
    core.wait_send()
    last.wait_send()
    for i in range(4):
        forward(c, i).wait_send()
    for k in range(1, 4):
        for o in range(3):
            for block in range(5):
                hop(0, block, o, k).wait_send()
                hop(1, block, o, k).wait_send()
            hop(2, 0, o, k).wait_send()


def hand_over(*refs):
    for i in range(4):
        refs[4 + i][...] = refs[i][...]


def body(
    tokens, grad_out, w_in, w_out, rel_bias, send_rows, recv_place, block_first, user_rows, stamps
):
    vmem, smem = pl.BlockSpec(memory_space=pltpu.VMEM), pl.BlockSpec(memory_space=pltpu.SMEM)
    hbm = pl.BlockSpec(memory_space=pl.ANY)
    dma = pltpu.SemaphoreType.DMA

    def v(shape, kind=BF16):
        return pltpu.VMEM(shape, kind)

    scratch = [
        v((4, 1024, 512)), v((1024, 512)), v((2048, 128), F32), v((64, 32, 128)),
        v((2, 64, 32, 128)), v((2, 2048, 128), F32), v((2, 8, 128), F32),
        v((8, 128, 128), F32), v((2, 128, 128), F32), v((256, 1024)), v((256, 1024)),
        v((1024, 256)), v((1024, 256)), v((4, 256, 512)), v((4, 256, 512), F32),
        v((8, 128, 128)), v((8, 128, 128), F32), v((256, 512), F32), v((256, 512), F32),
        v((2, 256, 128), F32), v((256, 512)), v((256, 512)), v((4, 256, 512)),
    ]
    scratch += [v((n, 4, 4, 4, 16, 128)) for n in COUNT]
    scratch += [v((3, n, 4, 4, 16, 128)) for n in COUNT]
    scratch += [v((n, 4, 4, 16, 128)) for n in COUNT]
    scratch += [v((3, n, 4, 16, 128)) for n in COUNT]
    scratch += [v((n, 4, 16, 128)) for n in COUNT]
    scratch += [v((3, n, 16, 128)) for n in COUNT]
    scratch += [
        v((20, 16, 128), F32), v((20, 8, 128), F32), v((2, 2, 2, 64, 1024), F32),
        v((2, 2, 64, 1024), F32), v((64, 32, 128)),
    ]
    scratch += [dma((5,)), dma((4,)), dma((4,)), dma((4,)), dma((4,))]
    scratch += [dma, dma, dma, dma, dma((45,)), dma((45,)), dma((45,)), dma((45,))]
    scratch += [dma((9,)), dma((9,)), dma, dma, dma, dma, dma((4,)), dma((4,))]
    results = pl.pallas_call(
            kernel,
            out_shape=(
                jax.ShapeDtypeStruct((128, 1024), BF16),
                jax.ShapeDtypeStruct((128, 1024), BF16),
                jax.ShapeDtypeStruct((8, 4096), F32),
                jax.ShapeDtypeStruct((8, 1024), F32),
            ),
            in_specs=[vmem, vmem, hbm, hbm, smem, vmem, vmem, smem, smem, vmem],
            out_specs=(vmem, vmem, vmem, vmem),
            scratch_shapes=scratch,
            compiler_params=pltpu.CompilerParams(
                collective_id=0, has_side_effects=True, vmem_limit_bytes=56 * 2**20
            ),
        )(
            tokens, grad_out, w_in, w_out, rel_bias, send_rows, recv_place, block_first,
            user_rows, stamps.reshape(1, 128),
        )
    return pl.pallas_call(
        hand_over,
        out_shape=tuple(jax.ShapeDtypeStruct(r.shape, r.dtype) for r in results),
        in_specs=[vmem] * 4,
        out_specs=(vmem,) * 4,
    )(*results)


def solution(mesh):
    placed = (
        P("seq", None), P("seq", None), P(), P(), P(), P("seq", None), P("seq", None),
        P("seq"), P("seq"), P("seq"),
    )
    return jax.shard_map(
        body,
        mesh=mesh,
        in_specs=placed,
        out_specs=(P("seq", None), P("seq", None), P("seq", None), P("seq", None)),
        check_vma=False,
    )
```

```python
import functools

import jax
import jax.numpy as jnp
from jax import lax
from jax.experimental import pallas as pl
from jax.experimental.pallas import tpu as pltpu
from jax.sharding import PartitionSpec as P

EPS = 1e-05
F32, BF16 = jnp.float32, jnp.bfloat16
MESH = pl.DeviceIdType.MESH
ORDERS = ((0, 0, 1, 2), (0, 1, 1, 2), (0, 1, 2, 2), (0, 0, 1, 2), (0, 1, 1, 2))
COUNT = tuple(sum(row.count(o) for row in ORDERS) for o in range(3))


def slots(block, order):
    start = sum(row.count(order) for row in ORDERS[:block])
    return start, ORDERS[block].count(order)


def dot(a, b, dims=((1,), (0,))):
    return lax.dot_general(a, b, (dims, ((), ())), preferred_element_type=F32)


def kernel(
    tok_in, gout_in, w_in, w_out, relb_in, srow_in, rplace_in, first, live, stamps_in,
    out, gx, gw1, gw2,
    tok, gout, relb, srow, rplace, stamps, wi, wo, sf, sa, rg, rf, meta, bias, mask, xv, gv, xt, gt, act, slp, pw, ps, mix, gg,
    stat, ga, gm, gp, b0, b1, b2, r10, r11, r12, h0, h1, h2, n0, n1, n2, s10, s11, s12, r20, r21, r22, s20, s21, s22,
    r30, r31, r32, fin, rfin, part, rpart, rz,
    in_sem, wsem, a_s, a_r, c_s, c_r, m_s, m_r, t_s, t_r, p1_s, p1_r, p2_s, p2_r, p3_s, p3_r,
    f_s, f_r, q_s, q_r, z_s, z_r,
):
    bs, r1, s1, r2 = (b0, b1, b2), (r10, r11, r12), (s10, s11, s12), (r20, r21, r22)
    halves, nears = (h0, h1, h2), (n0, n1, n2)
    s2, r3 = (s20, s21, s22), (r30, r31, r32)
    me = lax.axis_index("seq")
    c = lax.rem(me, 2)
    y = lax.rem(me // 2, 4)
    z = lax.rem(me // 8, 4)
    x = me // 32
    chip = me // 2
    mate = me + 1 - 2 * c
    coords, strides = (x, z, y), (32, 8, 2)

    def along(axis, k):
        there = lax.rem(coords[axis] + k, 4)
        return there, me + (there - coords[axis]) * strides[axis]

    def rcopy(src, dst, send, recv, dev):
        return pltpu.make_async_remote_copy(
            src_ref=src, dst_ref=dst, send_sem=send, recv_sem=recv,
            device_id=(dev,), device_id_type=MESH,
        )

    inputs = [
        pltpu.make_async_copy(src, dst, in_sem.at[i])
        for i, (src, dst) in enumerate(
            ((srow_in, srow), (tok_in, tok), (gout_in, gout), (rplace_in, rplace),
             (stamps_in, stamps), (relb_in, relb))
        )
    ]
    for load in inputs:
        load.start()
    barrier = pltpu.get_barrier_semaphore()

    pl.semaphore_signal(barrier, inc=1, device_id=(mate,), device_id_type=MESH)

    @pl.loop(1, 64)
    def _(k):
        pl.semaphore_signal(
            barrier, inc=1, device_id=(lax.rem(chip + k, 64) * 2 + c,), device_id_type=MESH
        )

    half = pl.multiple_of(c * 512, 512)
    loads = [
        pltpu.make_async_copy(w_in.at[:, pl.ds(f * 1024 + half, 512)], wi.at[f], wsem.at[f])
        for f in range(4)
    ]
    loads.append(pltpu.make_async_copy(w_out.at[:, pl.ds(half, 512)], wo, wsem.at[4]))

    rows = lax.broadcasted_iota(jnp.int32, (128, 128), 0)
    lanes = lax.broadcasted_iota(jnp.int32, (128, 128), 1)
    eye = rows == lanes

    def to_column(row):
        return jnp.sum(jnp.where(eye, row, 0.0), axis=1, keepdims=True)

    def to_row(column):
        return jnp.sum(jnp.where(eye, column, 0.0), axis=0, keepdims=True)

    for load in inputs:
        load.wait()
    order = ((rows & 63) << 1) + (rows >> 6)
    wanted = jnp.sum(
        jnp.where(lanes == order, srow[...].astype(F32), 0.0), axis=1, keepdims=True
    )
    pick = jnp.where(wanted == lanes.astype(F32), 1.0, 0.0).astype(BF16)

    def fold(value, kind, start=0):
        for o in range(2):
            for j in range(8):
                sf[kind, pl.ds(o * 8 + j, 64, stride=16), :] = value(
                    slice(64 * o, 64 * o + 64), slice(128 * j, 128 * j + 128)
                )
        sa[:, 16 * kind : 16 * kind + 16] = sf[kind].reshape(64, 16, 128).astype(BF16)

    def unfolded(ref, o):
        return jnp.concatenate(
            [ref[pl.ds(o * 8 + j, 64, stride=16), :] for j in range(8)], axis=1
        ).astype(BF16)

    picked = dot(pick, tok[...])
    fold(lambda at, cols: picked[at, cols], 0)

    pl.semaphore_wait(barrier, 64)

    def peer(i, j):
        there = lax.rem(x + i, 4) * 16 + lax.rem(z * 4 + y + j, 16)
        return there, there * 2 + c

    def scatter(rows, dst, sends, recvs):
        @pl.loop(0, 16)
        def _(j):
            for i in range(4):
                there, dev = peer(i, j)

                def go():
                    src = sa.at[there, rows]
                    rcopy(src, dst.at[chip], sends.at[i], recvs.at[i], dev).start()

                if i == 0:
                    pl.when(j > 0)(go)
                else:
                    go()

    def scattered(dst, sends, recvs, i):
        ref = dst.at[pl.ds(lax.rem(x + 4 - i, 4) * 16, 16 if i else 15)]
        return rcopy(ref, ref, sends.at[i], recvs.at[i], mate)

    def outward(kind, i):
        at = pl.ds(4 * kind, 4)
        return scattered(rg.at[kind, c], a_s.at[at], a_r.at[at], i)

    def leave(kind):
        rows, at = pl.ds(16 * kind, 16), pl.ds(4 * kind, 4)
        scatter(rows, rg.at[kind, c], a_s.at[at], a_r.at[at])
        rg[kind, c, chip] = sa[chip, rows]

    leave(0)
    picked_g = dot(pick, gout[...])
    fold(lambda at, cols: picked_g[at, cols], 1)
    leave(1)
    for load in loads:
        load.start()

    m = rplace[...]
    place = (m & 1) * 64 + (m >> 1)
    lands = place == rows
    slot = to_row(jnp.sum(jnp.where(lands, lanes.astype(F32), 0.0), axis=1, keepdims=True))
    when = to_row(jnp.sum(jnp.where(lands, stamps[...].astype(F32), 0.0), axis=1, keepdims=True))
    alive = slot < (live[0] + first[0] * 128).astype(F32)
    sub = lax.broadcasted_iota(jnp.int32, (8, 128), 0)
    meta[c] = jnp.where(
        sub == 0,
        jnp.where(alive, slot, 1e6),
        jnp.where(sub == 1, jnp.where(alive, slot, -1.0), when),
    )
    meta_copy = rcopy(meta.at[c], meta.at[c], m_s, m_r, mate)
    meta_copy.start()

    def wait_meta():
        rcopy(meta.at[1 - c], meta.at[1 - c], m_s, m_r, mate).wait_recv()

    wait_meta()
    for o in range(2):
        keys, asks, times = meta[o, 0:1], to_column(meta[o, 1:2]), meta[o, 2:3]
        mask[o] = jnp.where(keys <= asks, 1.0, 0.0)
        spread = to_column(times) - times

        @pl.loop(0, 4)
        def _(h, o=o, spread=spread):
            value = jnp.full((128, 128), relb[4 * c + h, 0], F32)
            for k in range(15):
                value = jnp.where(spread >= float(2**k), relb[4 * c + h, k + 1], value)
            bias[4 * o + h] = value

    def forward(kind, cs, i):
        at = pl.ds(lax.rem(x + 4 - i, 4) * 16, 16)
        ref = rg.at[kind, cs, at]
        return rcopy(ref, ref, c_s.at[4 * kind + i], c_r.at[4 * kind + i], mate)

    def widen(kind, cs, i):
        at = lax.rem(x + 4 - i, 4)
        wide = rg[kind, cs, pl.ds(at * 16, 16)].astype(F32).reshape(256, 128)
        rf[kind, cs, pl.ds(pl.multiple_of(at * 256, 256), 256)] = wide

    def arrive(kind):
        for i in (0, 1, 3, 2):
            outward(kind, i).wait_recv()
            forward(kind, c, i).start()
            widen(kind, c, i)

    def complete(kind, into):
        for i in (0, 1, 3, 2):
            forward(kind, 1 - c, i).wait_recv()
            widen(kind, 1 - c, i)
        for o in range(2):
            for cs in range(2):
                here = slice(128 * o + 64 * cs, 128 * o + 64 * cs + 64)
                into[here] = unfolded(rf.at[kind, cs], o)

    arrive(0)
    complete(0, xv)
    for load in loads:
        load.wait()

    def project(f):
        pre = dot(xv[...], wi[f])
        sig = jax.nn.sigmoid(pre)
        act[f] = (pre * sig).astype(BF16)
        slp[f] = sig * (1.0 + pre * (1.0 - sig))

    project(1)
    project(2)
    arrive(1)
    project(3)
    project(0)
    heads = [(o, h) for o in range(2) for h in range(4)]
    scale = 128**-0.5
    for o, h in heads:
        here = (slice(128 * o, 128 * o + 128), slice(128 * h, 128 * h + 128))
        v, q, k = (act[(f,) + here] for f in (1, 2, 3))
        logits = dot(q, k, ((1,), (1,))) * scale + bias[4 * o + h]
        sig = jax.nn.sigmoid(logits)
        allowed = mask[o] > 0.5
        w = jnp.where(allowed, logits * sig, 0.0).astype(BF16)
        pw[4 * o + h] = w
        ps[4 * o + h] = jnp.where(allowed, sig * (1.0 + logits * (1.0 - sig)), 0.0)
        mix[here] = dot(w, v)

    complete(1, gv)
    gg[...] = dot(gv[...], wo[...])

    gn = gg[...] * act[0].astype(F32)
    mixed = mix[...]
    total = jnp.sum(mixed, axis=1, keepdims=True)
    centre = mixed - total * (1.0 / 512)
    square = jnp.sum(centre * centre, axis=1, keepdims=True)
    gsum = jnp.sum(gn, axis=1, keepdims=True)
    gdot = jnp.sum(gn * centre, axis=1, keepdims=True)
    col = lax.broadcasted_iota(jnp.int32, (256, 128), 1)
    stat[c] = jnp.where(
        col == 0, total, jnp.where(col == 1, square, jnp.where(col == 2, gsum, gdot))
    )
    stat_copy = rcopy(stat.at[c], stat.at[c], t_s, t_r, mate)
    stat_copy.start()
    xt[...] = xv[...].T
    gt[...] = gv[...].T
    rcopy(stat.at[1 - c], stat.at[1 - c], t_s, t_r, mate).wait_recv()
    theirs = stat[1 - c]
    total2, square2, gsum2, gdot2 = (theirs[:, i : i + 1] for i in range(4))
    mean = (total + total2) * (1.0 / 1024)
    off, off2 = total * (1.0 / 512) - mean, total2 * (1.0 / 512) - mean
    var = (square + square2 + 512.0 * (off * off + off2 * off2)) * (1.0 / 1024)
    inv_std = lax.rsqrt(var + EPS)
    mean_gn = (gsum + gsum2) * (1.0 / 1024)
    mean_gnn = (gdot + off * gsum + gdot2 + off2 * gsum2) * inv_std * (1.0 / 1024)
    normed = (mix[...] - mean) * inv_std
    upper = act[0].astype(F32)
    ga[...] = (normed * upper).astype(BF16)
    ggv = gg[...]
    gm[...] = (inv_std * (ggv * upper - mean_gn - normed * mean_gnn)).astype(BF16)
    gp[0] = ((ggv * normed).astype(BF16).astype(F32) * slp[0]).astype(BF16)

    def product(block, left, right):
        @pl.loop(0, 4, unroll=True)
        def _(i):
            rows = pl.ds(pl.multiple_of(i * 256, 256), 256)
            tile = dot(left[rows, :], right).astype(BF16)
            seen = [0, 0, 0]
            for j in range(4):
                o = ORDERS[block][j]
                at = slots(block, o)[0] + seen[o]
                seen[o] += 1
                part4 = tile[:, 128 * j : 128 * j + 128].reshape(4, 4, 16, 128)
                if o == 0:
                    bs[0][at, i] = part4
                elif o == 1:
                    bs[1][at, :, :, i] = part4
                else:
                    for k in range(4):
                        bs[2][at, :, i, k] = part4[k]

    def tiles(block):
        return [(o, t) for o in range(3) for t in range(slots(block, o)[0], sum(slots(block, o)))]

    def near(step, o, t):
        here = coords[o]
        turn = 1 - 2 * lax.rem(here + t + c, 2)
        one, two = lax.rem(here + 4 + turn, 4), lax.rem(here + 4 - turn, 4)
        i = (sum(COUNT[:o]) + t) * 3
        sems = [(p1_s.at[i + n], p1_r.at[i + n]) for n in range(3)]
        if step == 0:
            dev = me + (one - here) * strides[o]
            return [
                rcopy(bs[o].at[t, quarter], r1[o].at[t, n], *sems[n], dev)
                for n, quarter in ((1, lax.rem(here + 2, 4)), (0, one))
            ]
        return two, rcopy(halves[o].at[t], nears[o].at[t], *sems[2], me + (two - here) * strides[o])

    def near_send(block):
        for o, t in tiles(block):
            for copy in near(0, o, t):
                copy.start()

    def near_pass(block):
        for o, t in tiles(block):
            near(0, o, t)[0].wait_recv()
            two, copy = near(1, o, t)
            halves[o][t] = (bs[o][t, two].astype(F32) + r1[o][t, 1].astype(F32)).astype(BF16)
            copy.start()

    def near_add(block):
        for o, t in tiles(block):
            near(0, o, t)[1].wait_recv()
            near(1, o, t)[1].wait_recv()
            value = bs[o][t, coords[o]].astype(F32) + r1[o][t, 0].astype(F32)
            s1[o][t] = (value + nears[o][t].astype(F32)).astype(BF16)

    def hop(stage, block, o, k):
        there, dev = along((o + stage) % 3, k)
        if stage == 1:
            start, count = slots(block, o)
            at = pl.ds(start, count)
            i = (block * 3 + o) * 3 + k - 1
            return rcopy(s1[o].at[at, there], r2[o].at[k - 1, at], p2_s.at[i], p2_r.at[i], dev)
        i = o * 3 + k - 1
        return rcopy(s2[o].at[:, there], r3[o].at[k - 1], p3_s.at[i], p3_r.at[i], dev)

    def far_send(block):
        near_add(block)
        for k in (2, 1, 3):
            for o in range(3):
                hop(1, block, o, k).start()

    def far_add(block):
        for o in range(3):
            for k in range(1, 4):
                hop(1, block, o, k).wait_recv()
            start, count = slots(block, o)
            at = slice(start, start + count)
            value = s1[o][at, coords[(o + 1) % 3]].astype(F32)
            for k in range(3):
                value = value + r2[o][k, at].astype(F32)
            s2[o][at] = value.astype(BF16)

    product(0, gt, ga[...])
    near_send(0)
    product(1, xt, gp[0])
    near_send(1)
    part[0] = dot(ga[...], wo[...], ((1,), (1,))).reshape(2, 2, 64, 1024)

    def across(kind):
        return rcopy(part.at[kind, :, 1 - c], rpart.at[kind], q_s.at[kind], q_r.at[kind], mate)

    def home(kind):
        across(kind).wait_recv()
        mine = pl.multiple_of(64 * c, 64)
        total = [part[kind, o, c] + rpart[kind, o] for o in range(2)]
        if kind:
            for o in range(2):
                total[o] = total[o] + gv[pl.ds(128 * o + mine, 64), :].astype(F32)
        for i in range(4):
            outward(kind, i).wait_send()
        fold(lambda at, cols: total[at.start // 64][:, cols], kind)

    across(0).start()

    for o, h in heads:
        here = (slice(128 * o, 128 * o + 128), slice(128 * h, 128 * h + 128))
        v, q, k = (act[(f,) + here] for f in (1, 2, 3))
        gmh, w = gm[here], pw[4 * o + h]
        gl = (dot(gmh, v, ((1,), (1,))) * ps[4 * o + h]).astype(BF16)
        grads = (
            dot(w, gmh, ((0,), (0,))),
            dot(gl, k) * scale,
            dot(gl, q, ((0,), (0,))) * scale,
        )
        for f in (1, 2, 3):
            gp[(f,) + here] = (
                grads[f - 1].astype(BF16).astype(F32) * slp[(f,) + here]
            ).astype(BF16)

    product(2, xt, gp[1])
    near_send(2)
    near_pass(0)
    product(3, xt, gp[2])
    near_send(3)
    near_pass(1)
    product(4, xt, gp[3])
    near_send(4)
    back = dot(gp[0], wi[0], ((1,), (1,)))
    for f in range(1, 4):
        back = back + dot(gp[f], wi[f], ((1,), (1,)))
    part[1] = back.reshape(2, 2, 64, 1024)
    across(1).start()
    near_pass(2)
    home(0)
    near_pass(3)
    home(1)
    near_pass(4)
    for block in range(5):
        far_send(block)
    scatter(pl.ds(0, 32), rz, z_s, z_r)
    rz[chip] = sa[chip]
    for block in range(5):
        far_add(block)
    for k in (2, 1, 3):
        for o in range(3):
            hop(2, 0, o, k).start()
    unpick = jnp.where(to_row(wanted) == rows.astype(F32), 1.0, 0.0).astype(BF16)

    for i in range(4):
        scattered(rz, z_s, z_r, i).wait_recv()

    def returned(kind):
        sf[kind] = rz[:, 16 * kind : 16 * kind + 16].astype(F32).reshape(1024, 128)
        return dot(
            unpick, jnp.concatenate([unfolded(sf.at[kind], o) for o in range(2)], axis=0)
        )

    out[...] = (tok[...].astype(F32) + returned(0)).astype(BF16)
    gx[...] = returned(1).astype(BF16)

    for o in range(3):
        for k in range(1, 4):
            hop(2, 0, o, k).wait_recv()
        value = s2[o][:, coords[(o + 2) % 3]].astype(F32)
        for k in range(3):
            value = value + r3[o][k].astype(F32)
        for block in range(5):
            start, _ = slots(block, o)
            mine = [j for j in range(4) if ORDERS[block][j] == o]
            for n, j in enumerate(mine):
                fin[4 * block + j] = value[start + n]
    away, home = pl.multiple_of(8 * (1 - c), 8), pl.multiple_of(8 * c, 8)
    last = rcopy(fin.at[:, pl.ds(away, 8)], rfin, f_s, f_r, mate)
    last.start()
    other = pl.multiple_of(512 - half, 512)
    mine = fin[:, pl.ds(home, 8)]
    for j in range(4):
        gw2[:, pl.ds(half + 128 * j, 128)] = mine[j]
        for f in range(4):
            gw1[:, pl.ds(f * 1024 + half + 128 * j, 128)] = mine[4 + 4 * f + j]
    last.wait_recv()
    for j in range(4):
        gw2[:, pl.ds(other + 128 * j, 128)] = rfin[j]
        for f in range(4):
            gw1[:, pl.ds(f * 1024 + other + 128 * j, 128)] = rfin[4 + 4 * f + j]

    for i in range(4):
        scattered(rz, z_s, z_r, i).wait_send()
        for kind in range(2):
            forward(kind, c, i).wait_send()
    for kind in range(2):
        across(kind).wait_send()
    meta_copy.wait_send()
    stat_copy.wait_send()
    last.wait_send()
    for k in range(1, 4):
        for o in range(3):
            for block in range(5):
                hop(1, block, o, k).wait_send()
            hop(2, 0, o, k).wait_send()
    for block in range(5):
        for o, t in tiles(block):
            for copy in near(0, o, t) + [near(1, o, t)[1]]:
                copy.wait_send()


def hand_over(*refs):
    for i in range(4):
        refs[4 + i][...] = refs[i][...]


def body(
    tokens, grad_out, w_in, w_out, rel_bias, send_rows, recv_place, block_first, user_rows, stamps
):
    vmem, smem = pl.BlockSpec(memory_space=pltpu.VMEM), pl.BlockSpec(memory_space=pltpu.SMEM)
    hbm = pl.BlockSpec(memory_space=pl.ANY)
    dma = pltpu.SemaphoreType.DMA

    def v(shape, kind=BF16):
        return pltpu.VMEM(shape, kind)

    scratch = [
        v((128, 1024)), v((128, 1024)), pltpu.SMEM((8, 16), F32), v((1, 128), jnp.int32),
        v((1, 128), jnp.int32), v((1, 128), jnp.int32),
        v((4, 1024, 512)), v((1024, 512)), v((2, 1024, 128), F32), v((64, 32, 128)),
        v((2, 2, 64, 16, 128)), v((2, 2, 1024, 128), F32), v((2, 8, 128), F32),
        v((8, 128, 128), F32), v((2, 128, 128), F32), v((256, 1024)), v((256, 1024)),
        v((1024, 256)), v((1024, 256)), v((4, 256, 512)), v((4, 256, 512), F32),
        v((8, 128, 128)), v((8, 128, 128), F32), v((256, 512), F32), v((256, 512), F32),
        v((2, 256, 128), F32), v((256, 512)), v((256, 512)), v((4, 256, 512)),
    ]
    scratch += [v((n, 4, 4, 4, 16, 128)) for n in COUNT]
    scratch += [v((n, 2, 4, 4, 16, 128)) for n in COUNT]
    scratch += [v((n, 4, 4, 16, 128)) for n in COUNT]
    scratch += [v((n, 4, 4, 16, 128)) for n in COUNT]
    scratch += [v((n, 4, 4, 16, 128)) for n in COUNT]
    scratch += [v((3, n, 4, 16, 128)) for n in COUNT]
    scratch += [v((n, 4, 16, 128)) for n in COUNT]
    scratch += [v((3, n, 16, 128)) for n in COUNT]
    scratch += [
        v((20, 16, 128), F32), v((20, 8, 128), F32), v((2, 2, 2, 64, 1024), F32),
        v((2, 2, 64, 1024), F32), v((64, 32, 128)),
    ]
    scratch += [dma((6,)), dma((5,)), dma((8,)), dma((8,)), dma((8,)), dma((8,))]
    scratch += [dma, dma, dma, dma, dma((60,)), dma((60,)), dma((45,)), dma((45,))]
    scratch += [dma((9,)), dma((9,)), dma, dma, dma((2,)), dma((2,)), dma((4,)), dma((4,))]
    results = pl.pallas_call(
            kernel,
            out_shape=(
                jax.ShapeDtypeStruct((128, 1024), BF16),
                jax.ShapeDtypeStruct((128, 1024), BF16),
                jax.ShapeDtypeStruct((8, 4096), F32),
                jax.ShapeDtypeStruct((8, 1024), F32),
            ),
            in_specs=[hbm] * 7 + [smem, smem, hbm],
            out_specs=(vmem, vmem, vmem, vmem),
            scratch_shapes=scratch,
            compiler_params=pltpu.CompilerParams(
                collective_id=0, has_side_effects=True, vmem_limit_bytes=56 * 2**20
            ),
        )(
            tokens, grad_out, w_in, w_out, rel_bias, send_rows, recv_place, block_first,
            user_rows, stamps.reshape(1, 128),
        )
    return pl.pallas_call(
        hand_over,
        out_shape=tuple(jax.ShapeDtypeStruct(r.shape, r.dtype) for r in results),
        in_specs=[vmem] * 4,
        out_specs=(vmem,) * 4,
    )(*results)


def solution(mesh):
    placed = (
        P("seq", None), P("seq", None), P(), P(), P(), P("seq", None), P("seq", None),
        P("seq"), P("seq"), P("seq"),
    )
    return jax.shard_map(
        body,
        mesh=mesh,
        in_specs=placed,
        out_specs=(P("seq", None), P("seq", None), P("seq", None), P("seq", None)),
        check_vma=False,
    )
```

```python
import functools

import jax
import jax.numpy as jnp
from jax import lax
from jax.experimental import pallas as pl
from jax.experimental.pallas import tpu as pltpu
from jax.sharding import PartitionSpec as P

EPS = 1e-05
F32, BF16 = jnp.float32, jnp.bfloat16
MESH = pl.DeviceIdType.MESH
ORDERS = ((0, 0, 1, 2), (0, 1, 1, 2), (0, 1, 2, 2), (0, 0, 1, 2), (0, 1, 1, 2))
COUNT = tuple(sum(row.count(o) for row in ORDERS) for o in range(3))


def slots(block, order):
    start = sum(row.count(order) for row in ORDERS[:block])
    return start, ORDERS[block].count(order)


def dot(a, b, dims=((1,), (0,))):
    return lax.dot_general(a, b, (dims, ((), ())), preferred_element_type=F32)


def kernel(
    tok_in, gout_in, w_in, w_out, relb_in, srow_in, rplace_in, first, live, stamps_in,
    out, gx, gw1, gw2,
    tok, gout, relb, srow, rplace, stamps, wi, wo, sf, sa, rg, rf, meta, bias, mask, xv, gv, xt, gt, act, slp, pw, ps, mix, gg,
    stat, ga, gm, gp, b0, b1, b2, r10, r11, r12, h0, h1, h2, n0, n1, n2, s10, s11, s12, r20, r21, r22, s20, s21, s22,
    r30, r31, r32, fin, rfin, part, rpart, rz, xn, yn,
    in_sem, wsem, a_s, a_r, c_s, c_r, m_s, m_r, t_s, t_r, p1_s, p1_r, p2_s, p2_r, p3_s, p3_r,
    f_s, f_r, q_s, q_r, z_s, z_r, e_s, e_r,
):
    bs, r1, s1, r2 = (b0, b1, b2), (r10, r11, r12), (s10, s11, s12), (r20, r21, r22)
    halves, nears = (h0, h1, h2), (n0, n1, n2)
    s2, r3 = (s20, s21, s22), (r30, r31, r32)
    me = lax.axis_index("seq")
    c = lax.rem(me, 2)
    y = lax.rem(me // 2, 4)
    z = lax.rem(me // 8, 4)
    x = me // 32
    chip = me // 2
    mate = me + 1 - 2 * c
    coords, strides = (x, z, y), (32, 8, 2)

    def along(axis, k):
        there = lax.rem(coords[axis] + k, 4)
        return there, me + (there - coords[axis]) * strides[axis]

    def rcopy(src, dst, send, recv, dev):
        return pltpu.make_async_remote_copy(
            src_ref=src, dst_ref=dst, send_sem=send, recv_sem=recv,
            device_id=(dev,), device_id_type=MESH,
        )

    inputs = [
        pltpu.make_async_copy(src, dst, in_sem.at[i])
        for i, (src, dst) in enumerate(
            ((srow_in, srow), (tok_in, tok), (gout_in, gout), (rplace_in, rplace),
             (stamps_in, stamps), (relb_in, relb))
        )
    ]
    for load in inputs:
        load.start()
    barrier = pltpu.get_barrier_semaphore()

    pl.semaphore_signal(barrier, inc=1, device_id=(mate,), device_id_type=MESH)

    @pl.loop(1, 64)
    def _(k):
        pl.semaphore_signal(
            barrier, inc=1, device_id=(lax.rem(chip + k, 64) * 2 + c,), device_id_type=MESH
        )

    half = pl.multiple_of(c * 512, 512)
    loads = [
        pltpu.make_async_copy(w_in.at[:, pl.ds(f * 1024 + half, 512)], wi.at[f], wsem.at[f])
        for f in range(4)
    ]
    loads.append(pltpu.make_async_copy(w_out.at[:, pl.ds(half, 512)], wo, wsem.at[4]))

    rows = lax.broadcasted_iota(jnp.int32, (128, 128), 0)
    lanes = lax.broadcasted_iota(jnp.int32, (128, 128), 1)
    eye = rows == lanes

    def to_column(row):
        return jnp.sum(jnp.where(eye, row, 0.0), axis=1, keepdims=True)

    def to_row(column):
        return jnp.sum(jnp.where(eye, column, 0.0), axis=0, keepdims=True)

    for load in inputs:
        load.wait()
    order = ((rows & 63) << 1) + (rows >> 6)
    wanted = jnp.sum(
        jnp.where(lanes == order, srow[...].astype(F32), 0.0), axis=1, keepdims=True
    )
    pick = jnp.where(wanted == lanes.astype(F32), 1.0, 0.0).astype(BF16)

    def fold(value, kind, start=0):
        for o in range(2):
            for j in range(8):
                sf[kind, pl.ds(o * 8 + j, 64, stride=16), :] = value(
                    slice(64 * o, 64 * o + 64), slice(128 * j, 128 * j + 128)
                )
        sa[:, 16 * kind : 16 * kind + 16] = sf[kind].reshape(64, 16, 128).astype(BF16)

    def unfolded(ref, o):
        return jnp.concatenate(
            [ref[pl.ds(o * 8 + j, 64, stride=16), :] for j in range(8)], axis=1
        ).astype(BF16)

    picked = dot(pick, tok[...])
    fold(lambda at, cols: picked[at, cols], 0)

    pl.semaphore_wait(barrier, 64)

    def peer(i, j):
        there = lax.rem(x + i, 4) * 16 + lax.rem(z * 4 + y + j, 16)
        return there, there * 2 + c

    def scatter(rows, dst, sends, recvs):
        @pl.loop(0, 16)
        def _(j):
            for i in range(4):
                there, dev = peer(i, j)

                def go():
                    src = sa.at[there, rows]
                    rcopy(src, dst.at[chip], sends.at[i], recvs.at[i], dev).start()

                if i == 0:
                    pl.when(j > 0)(go)
                else:
                    go()

    def scattered(dst, sends, recvs, i):
        ref = dst.at[pl.ds(lax.rem(x + 4 - i, 4) * 16, 16 if i else 15)]
        return rcopy(ref, ref, sends.at[i], recvs.at[i], mate)

    def outward(kind, i):
        at = pl.ds(4 * kind, 4)
        return scattered(rg.at[kind, c], a_s.at[at], a_r.at[at], i)

    def leave(kind):
        rows, at = pl.ds(16 * kind, 16), pl.ds(4 * kind, 4)
        scatter(rows, rg.at[kind, c], a_s.at[at], a_r.at[at])
        rg[kind, c, chip] = sa[chip, rows]

    leave(0)
    picked_g = dot(pick, gout[...])
    fold(lambda at, cols: picked_g[at, cols], 1)
    leave(1)
    for load in loads:
        load.start()

    m = rplace[...]
    place = (m & 1) * 64 + (m >> 1)
    lands = place == rows
    slot = to_row(jnp.sum(jnp.where(lands, lanes.astype(F32), 0.0), axis=1, keepdims=True))
    when = to_row(jnp.sum(jnp.where(lands, stamps[...].astype(F32), 0.0), axis=1, keepdims=True))
    alive = slot < (live[0] + first[0] * 128).astype(F32)
    sub = lax.broadcasted_iota(jnp.int32, (8, 128), 0)
    meta[c] = jnp.where(
        sub == 0,
        jnp.where(alive, slot, 1e6),
        jnp.where(sub == 1, jnp.where(alive, slot, -1.0), when),
    )
    meta_copy = rcopy(meta.at[c], meta.at[c], m_s, m_r, mate)
    meta_copy.start()

    def wait_meta():
        rcopy(meta.at[1 - c], meta.at[1 - c], m_s, m_r, mate).wait_recv()

    wait_meta()
    for o in range(2):
        keys, asks, times = meta[o, 0:1], to_column(meta[o, 1:2]), meta[o, 2:3]
        mask[o] = jnp.where(keys <= asks, 1.0, 0.0)
        spread = to_column(times) - times

        @pl.loop(0, 4)
        def _(h, o=o, spread=spread):
            value = jnp.full((128, 128), relb[4 * c + h, 0], F32)
            for k in range(15):
                value = jnp.where(spread >= float(2**k), relb[4 * c + h, k + 1], value)
            bias[4 * o + h] = value

    def forward(kind, cs, i):
        at = pl.ds(lax.rem(x + 4 - i, 4) * 16, 16)
        ref = rg.at[kind, cs, at]
        return rcopy(ref, ref, c_s.at[4 * kind + i], c_r.at[4 * kind + i], mate)

    def widen(kind, cs, i):
        at = lax.rem(x + 4 - i, 4)
        wide = rg[kind, cs, pl.ds(at * 16, 16)].astype(F32).reshape(256, 128)
        rf[kind, cs, pl.ds(pl.multiple_of(at * 256, 256), 256)] = wide

    def arrive(kind):
        for i in (0, 1, 3, 2):
            outward(kind, i).wait_recv()
            forward(kind, c, i).start()
            widen(kind, c, i)

    def complete(kind, into):
        for i in (0, 1, 3, 2):
            forward(kind, 1 - c, i).wait_recv()
            widen(kind, 1 - c, i)
        for o in range(2):
            for cs in range(2):
                here = slice(128 * o + 64 * cs, 128 * o + 64 * cs + 64)
                into[here] = unfolded(rf.at[kind, cs], o)

    arrive(0)
    complete(0, xv)

    def pair(o, e):
        here = coords[o]
        turn = 1 - 2 * lax.rem(here + e + c, 2)
        one, two = lax.rem(here + 4 + turn, 4), lax.rem(here + 4 - turn, 4)
        to_one, to_two = (me + (n - here) * strides[o] for n in (one, two))
        return here, lax.rem(here + 2, 4), one, two, to_one, to_two

    def quarter(ref, o, q):
        return ref.at[(slice(None),) * o + (q,)]

    def early(o, e):
        _, across, one, _, dev, _ = pair(o, e)
        i = (o * 2 + e) * 2
        return [
            rcopy(quarter(xt, o, q), xn.at[o, e, n], e_s.at[i + n], e_r.at[i + n], dev)
            for n, q in ((1, across), (0, one))
        ]

    xt[...] = xv[...].T.reshape(4, 4, 4, 16, 256)
    for e in range(2):
        for o in range(3):
            for copy in early(o, e):
                copy.start()
    for load in loads:
        load.wait()

    def project(f):
        pre = dot(xv[...], wi[f])
        sig = jax.nn.sigmoid(pre)
        act[f] = (pre * sig).astype(BF16)
        slp[f] = sig * (1.0 + pre * (1.0 - sig))

    project(1)
    project(2)
    arrive(1)
    project(3)
    project(0)
    heads = [(o, h) for o in range(2) for h in range(4)]
    scale = 128**-0.5
    for o, h in heads:
        here = (slice(128 * o, 128 * o + 128), slice(128 * h, 128 * h + 128))
        v, q, k = (act[(f,) + here] for f in (1, 2, 3))
        logits = dot(q, k, ((1,), (1,))) * scale + bias[4 * o + h]
        sig = jax.nn.sigmoid(logits)
        allowed = mask[o] > 0.5
        w = jnp.where(allowed, logits * sig, 0.0).astype(BF16)
        pw[4 * o + h] = w
        ps[4 * o + h] = jnp.where(allowed, sig * (1.0 + logits * (1.0 - sig)), 0.0)
        mix[here] = dot(w, v)

    complete(1, gv)
    gg[...] = dot(gv[...], wo[...])

    gn = gg[...] * act[0].astype(F32)
    mixed = mix[...]
    total = jnp.sum(mixed, axis=1, keepdims=True)
    centre = mixed - total * (1.0 / 512)
    square = jnp.sum(centre * centre, axis=1, keepdims=True)
    gsum = jnp.sum(gn, axis=1, keepdims=True)
    gdot = jnp.sum(gn * centre, axis=1, keepdims=True)
    col = lax.broadcasted_iota(jnp.int32, (256, 128), 1)
    stat[c] = jnp.where(
        col == 0, total, jnp.where(col == 1, square, jnp.where(col == 2, gsum, gdot))
    )
    stat_copy = rcopy(stat.at[c], stat.at[c], t_s, t_r, mate)
    stat_copy.start()
    gt[...] = gv[...].T.reshape(4, 4, 4, 16, 256)
    rcopy(stat.at[1 - c], stat.at[1 - c], t_s, t_r, mate).wait_recv()
    theirs = stat[1 - c]
    total2, square2, gsum2, gdot2 = (theirs[:, i : i + 1] for i in range(4))
    mean = (total + total2) * (1.0 / 1024)
    off, off2 = total * (1.0 / 512) - mean, total2 * (1.0 / 512) - mean
    var = (square + square2 + 512.0 * (off * off + off2 * off2)) * (1.0 / 1024)
    inv_std = lax.rsqrt(var + EPS)
    mean_gn = (gsum + gsum2) * (1.0 / 1024)
    mean_gnn = (gdot + off * gsum + gdot2 + off2 * gsum2) * inv_std * (1.0 / 1024)
    normed = (mix[...] - mean) * inv_std
    upper = act[0].astype(F32)
    ga[...] = (normed * upper).astype(BF16)
    ggv = gg[...]
    gm[...] = (inv_std * (ggv * upper - mean_gn - normed * mean_gnn)).astype(BF16)
    gp[0] = ((ggv * normed).astype(BF16).astype(F32) * slp[0]).astype(BF16)

    def product(block, left, right):
        @pl.loop(0, 4, unroll=True)
        def _(i):
            tile = dot(left[i].reshape(256, 256), right).astype(BF16)
            seen = [0, 0, 0]
            for j in range(4):
                o = ORDERS[block][j]
                at = slots(block, o)[0] + seen[o]
                seen[o] += 1
                part4 = tile[:, 128 * j : 128 * j + 128].reshape(4, 4, 16, 128)
                if o == 0:
                    bs[0][at, i] = part4
                elif o == 1:
                    bs[1][at, :, :, i] = part4
                else:
                    for k in range(4):
                        bs[2][at, :, i, k] = part4[k]

    def tiles(block):
        return [(o, t) for o in range(3) for t in range(slots(block, o)[0], sum(slots(block, o)))]

    def near(step, o, t):
        _, across, one, two, dev, dev2 = pair(o, t % 2)
        i = (sum(COUNT[:o]) + t) * 3
        sems = [(p1_s.at[i + n], p1_r.at[i + n]) for n in range(3)]
        if step == 0:
            return [
                rcopy(bs[o].at[t, q], r1[o].at[t, n], *sems[n], dev)
                for n, q in ((1, across), (0, one))
            ]
        return two, rcopy(halves[o].at[t], nears[o].at[t], *sems[2], dev2)

    def swap(block, o, t):
        j = [j for j in range(4) if ORDERS[block][j] == o][t - slots(block, o)[0]]
        i = sum(COUNT[:o]) + t
        mine, theirs = gp.at[block - 1, :, pl.ds(128 * j, 128)], yn.at[i]
        return mine, theirs, rcopy(mine, theirs, p1_s.at[3 * i], p1_r.at[3 * i], pair(o, t % 2)[4])

    def near_send(block):
        for o, t in tiles(block):
            for copy in near(0, o, t) if block < 2 else [swap(block, o, t)[2]]:
                copy.start()

    came = set()

    def near_pass(block):
        for o, t in tiles(block):
            e = t % 2
            here, _, _, two, _, _ = pair(o, e)
            copy = near(1, o, t)[1]
            if block < 2:
                near(0, o, t)[0].wait_recv()
                halves[o][t] = (bs[o][t, two].astype(F32) + r1[o][t, 1].astype(F32)).astype(BF16)
                copy.start()
                continue
            if (o, e) not in came:
                came.add((o, e))
                for arrival in early(o, e):
                    arrival.wait_recv()
            mine, theirs, swapped = swap(block, o, t)
            swapped.wait_recv()
            for n, q in ((1, two), (0, here)):
                left = quarter(xt, o, q)[...].reshape(256, 256)
                value = dot(left, mine[...]) + dot(xn[o, e, n].reshape(256, 256), theirs[...])
                value = value.astype(BF16).reshape(4, 4, 16, 128)
                into = halves[o].at[t] if n else bs[o].at[t, here]
                if o == 1:
                    for k in range(4):
                        into[:, k] = value[k]
                else:
                    into[...] = value
                if n:
                    copy.start()

    def near_add(block):
        for o, t in tiles(block):
            near(1, o, t)[1].wait_recv()
            value = bs[o][t, coords[o]].astype(F32) + nears[o][t].astype(F32)
            if block < 2:
                near(0, o, t)[1].wait_recv()
                value = value + r1[o][t, 0].astype(F32)
            s1[o][t] = value.astype(BF16)

    def hop(stage, block, o, k):
        there, dev = along((o + stage) % 3, k)
        if stage == 1:
            start, count = slots(block, o)
            at = pl.ds(start, count)
            i = (block * 3 + o) * 3 + k - 1
            return rcopy(s1[o].at[at, there], r2[o].at[k - 1, at], p2_s.at[i], p2_r.at[i], dev)
        i = o * 3 + k - 1
        return rcopy(s2[o].at[:, there], r3[o].at[k - 1], p3_s.at[i], p3_r.at[i], dev)

    def far_send(block):
        near_add(block)
        for k in (2, 1, 3):
            for o in range(3):
                hop(1, block, o, k).start()

    def far_add(block):
        for o in range(3):
            for k in range(1, 4):
                hop(1, block, o, k).wait_recv()
            start, count = slots(block, o)
            at = slice(start, start + count)
            value = s1[o][at, coords[(o + 1) % 3]].astype(F32)
            for k in range(3):
                value = value + r2[o][k, at].astype(F32)
            s2[o][at] = value.astype(BF16)

    product(0, gt, ga[...])
    near_send(0)
    product(1, xt, gp[0])
    near_send(1)
    part[0] = dot(ga[...], wo[...], ((1,), (1,))).reshape(2, 2, 64, 1024)

    def across(kind):
        return rcopy(part.at[kind, :, 1 - c], rpart.at[kind], q_s.at[kind], q_r.at[kind], mate)

    def home(kind):
        across(kind).wait_recv()
        mine = pl.multiple_of(64 * c, 64)
        total = [part[kind, o, c] + rpart[kind, o] for o in range(2)]
        if kind:
            for o in range(2):
                total[o] = total[o] + gv[pl.ds(128 * o + mine, 64), :].astype(F32)
        for i in range(4):
            outward(kind, i).wait_send()
        fold(lambda at, cols: total[at.start // 64][:, cols], kind)

    across(0).start()

    for o, h in heads:
        here = (slice(128 * o, 128 * o + 128), slice(128 * h, 128 * h + 128))
        v, q, k = (act[(f,) + here] for f in (1, 2, 3))
        gmh, w = gm[here], pw[4 * o + h]
        gl = (dot(gmh, v, ((1,), (1,))) * ps[4 * o + h]).astype(BF16)
        grads = (
            dot(w, gmh, ((0,), (0,))),
            dot(gl, k) * scale,
            dot(gl, q, ((0,), (0,))) * scale,
        )
        for f in (1, 2, 3):
            gp[(f,) + here] = (
                grads[f - 1].astype(BF16).astype(F32) * slp[(f,) + here]
            ).astype(BF16)

    for block in range(2, 5):
        near_send(block)
    near_pass(0)
    near_pass(1)
    back = dot(gp[0], wi[0], ((1,), (1,)))
    for f in range(1, 4):
        back = back + dot(gp[f], wi[f], ((1,), (1,)))
    part[1] = back.reshape(2, 2, 64, 1024)
    across(1).start()
    near_pass(2)
    near_pass(3)
    near_pass(4)
    far_send(0)
    far_send(1)
    home(0)
    home(1)
    for block in range(2, 5):
        far_send(block)
    scatter(pl.ds(0, 32), rz, z_s, z_r)
    rz[chip] = sa[chip]
    for block in range(5):
        far_add(block)
    for k in (2, 1, 3):
        for o in range(3):
            hop(2, 0, o, k).start()
    for o in range(3):
        for k in range(1, 4):
            hop(2, 0, o, k).wait_recv()
        value = s2[o][:, coords[(o + 2) % 3]].astype(F32)
        for k in range(3):
            value = value + r3[o][k].astype(F32)
        for block in range(5):
            start, _ = slots(block, o)
            mine = [j for j in range(4) if ORDERS[block][j] == o]
            for n, j in enumerate(mine):
                fin[4 * block + j] = value[start + n]
    away, home = pl.multiple_of(8 * (1 - c), 8), pl.multiple_of(8 * c, 8)
    last = rcopy(fin.at[:, pl.ds(away, 8)], rfin, f_s, f_r, mate)
    last.start()
    unpick = jnp.where(to_row(wanted) == rows.astype(F32), 1.0, 0.0).astype(BF16)

    for i in range(4):
        scattered(rz, z_s, z_r, i).wait_recv()

    def returned(kind):
        sf[kind] = rz[:, 16 * kind : 16 * kind + 16].astype(F32).reshape(1024, 128)
        return dot(
            unpick, jnp.concatenate([unfolded(sf.at[kind], o) for o in range(2)], axis=0)
        )

    out[...] = (tok[...].astype(F32) + returned(0)).astype(BF16)
    gx[...] = returned(1).astype(BF16)

    other = pl.multiple_of(512 - half, 512)
    mine = fin[:, pl.ds(home, 8)]
    for j in range(4):
        gw2[:, pl.ds(half + 128 * j, 128)] = mine[j]
        for f in range(4):
            gw1[:, pl.ds(f * 1024 + half + 128 * j, 128)] = mine[4 + 4 * f + j]
    last.wait_recv()
    for j in range(4):
        gw2[:, pl.ds(other + 128 * j, 128)] = rfin[j]
        for f in range(4):
            gw1[:, pl.ds(f * 1024 + other + 128 * j, 128)] = rfin[4 + 4 * f + j]

    for i in range(4):
        scattered(rz, z_s, z_r, i).wait_send()
        for kind in range(2):
            forward(kind, c, i).wait_send()
    for kind in range(2):
        across(kind).wait_send()
    meta_copy.wait_send()
    stat_copy.wait_send()
    last.wait_send()
    for k in range(1, 4):
        for o in range(3):
            for block in range(5):
                hop(1, block, o, k).wait_send()
            hop(2, 0, o, k).wait_send()
    for block in range(5):
        for o, t in tiles(block):
            near(1, o, t)[1].wait_send()
            for copy in near(0, o, t) if block < 2 else [swap(block, o, t)[2]]:
                copy.wait_send()
    for e in range(2):
        for o in range(3):
            for copy in early(o, e):
                copy.wait_send()


def hand_over(*refs):
    for i in range(4):
        refs[4 + i][...] = refs[i][...]


def body(
    tokens, grad_out, w_in, w_out, rel_bias, send_rows, recv_place, block_first, user_rows, stamps
):
    vmem, smem = pl.BlockSpec(memory_space=pltpu.VMEM), pl.BlockSpec(memory_space=pltpu.SMEM)
    hbm = pl.BlockSpec(memory_space=pl.ANY)
    dma = pltpu.SemaphoreType.DMA

    def v(shape, kind=BF16):
        return pltpu.VMEM(shape, kind)

    scratch = [
        v((128, 1024)), v((128, 1024)), pltpu.SMEM((8, 16), F32), v((1, 128), jnp.int32),
        v((1, 128), jnp.int32), v((1, 128), jnp.int32),
        v((4, 1024, 512)), v((1024, 512)), v((2, 1024, 128), F32), v((64, 32, 128)),
        v((2, 2, 64, 16, 128)), v((2, 2, 1024, 128), F32), v((2, 8, 128), F32),
        v((8, 128, 128), F32), v((2, 128, 128), F32), v((256, 1024)), v((256, 1024)),
        v((4, 4, 4, 16, 256)), v((4, 4, 4, 16, 256)), v((4, 256, 512)), v((4, 256, 512), F32),
        v((8, 128, 128)), v((8, 128, 128), F32), v((256, 512), F32), v((256, 512), F32),
        v((2, 256, 128), F32), v((256, 512)), v((256, 512)), v((4, 256, 512)),
    ]
    scratch += [v((n, 4, 4, 4, 16, 128)) for n in COUNT]
    scratch += [v((n, 2, 4, 4, 16, 128)) for n in COUNT]
    scratch += [v((n, 4, 4, 16, 128)) for n in COUNT]
    scratch += [v((n, 4, 4, 16, 128)) for n in COUNT]
    scratch += [v((n, 4, 4, 16, 128)) for n in COUNT]
    scratch += [v((3, n, 4, 16, 128)) for n in COUNT]
    scratch += [v((n, 4, 16, 128)) for n in COUNT]
    scratch += [v((3, n, 16, 128)) for n in COUNT]
    scratch += [
        v((20, 16, 128), F32), v((20, 8, 128), F32), v((2, 2, 2, 64, 1024), F32),
        v((2, 2, 64, 1024), F32), v((64, 32, 128)), v((3, 2, 2, 4, 4, 16, 256)),
        v((20, 256, 128)),
    ]
    scratch += [dma((6,)), dma((5,)), dma((8,)), dma((8,)), dma((8,)), dma((8,))]
    scratch += [dma, dma, dma, dma, dma((60,)), dma((60,)), dma((45,)), dma((45,))]
    scratch += [dma((9,)), dma((9,)), dma, dma, dma((2,)), dma((2,)), dma((4,)), dma((4,))]
    scratch += [dma((12,)), dma((12,))]
    results = pl.pallas_call(
            kernel,
            out_shape=(
                jax.ShapeDtypeStruct((128, 1024), BF16),
                jax.ShapeDtypeStruct((128, 1024), BF16),
                jax.ShapeDtypeStruct((8, 4096), F32),
                jax.ShapeDtypeStruct((8, 1024), F32),
            ),
            in_specs=[hbm] * 7 + [smem, smem, hbm],
            out_specs=(vmem, vmem, vmem, vmem),
            scratch_shapes=scratch,
            compiler_params=pltpu.CompilerParams(
                collective_id=0, has_side_effects=True, vmem_limit_bytes=56 * 2**20
            ),
        )(
            tokens, grad_out, w_in, w_out, rel_bias, send_rows, recv_place, block_first,
            user_rows, stamps.reshape(1, 128),
        )
    return pl.pallas_call(
        hand_over,
        out_shape=tuple(jax.ShapeDtypeStruct(r.shape, r.dtype) for r in results),
        in_specs=[vmem] * 4,
        out_specs=(vmem,) * 4,
    )(*results)


def solution(mesh):
    placed = (
        P("seq", None), P("seq", None), P(), P(), P(), P("seq", None), P("seq", None),
        P("seq"), P("seq"), P("seq"),
    )
    return jax.shard_map(
        body,
        mesh=mesh,
        in_specs=placed,
        out_specs=(P("seq", None), P("seq", None), P("seq", None), P("seq", None)),
        check_vma=False,
    )
```

```python
import functools

import jax
import jax.numpy as jnp
from jax import lax
from jax.experimental import pallas as pl
from jax.experimental.pallas import tpu as pltpu
from jax.sharding import PartitionSpec as P

EPS = 1e-05
F32, BF16 = jnp.float32, jnp.bfloat16
MESH = pl.DeviceIdType.MESH
ORDERS = ((0, 0, 1, 2), (0, 1, 1, 2), (0, 1, 2, 2), (0, 0, 1, 2), (0, 1, 1, 2))
COUNT = tuple(sum(row.count(o) for row in ORDERS) for o in range(3))
PAIRS = tuple((n + 1) // 2 for n in COUNT)


def slots(block, order):
    start = sum(row.count(order) for row in ORDERS[:block])
    return start, ORDERS[block].count(order)


def dot(a, b, dims=((1,), (0,))):
    return lax.dot_general(a, b, (dims, ((), ())), preferred_element_type=F32)


def kernel(
    tok_in, gout_in, w_in, w_out, relb_in, srow_in, rplace_in, first, live, stamps_in,
    out, gx, gw1, gw2,
    tok, gout, relb, srow, rplace, stamps, wi, wo, sf, sa, rg, rf, meta, bias, mask, xv, gv, xt, gt, act, slp, pw, ps, mix, gg,
    stat, ga, gm, gp, b0, b1, b2, r10, r11, r12, h0, h1, h2, n0, n1, n2, s10, s11, s12, r20, r21, r22, s20, s21, s22,
    r30, r31, r32, k20, k21, k22, part, rpart, rz, xn, yn,
    in_sem, wsem, a_s, a_r, c_s, c_r, m_s, m_r, t_s, t_r, p1_s, p1_r, p2_s, p2_r, p3_s, p3_r,
    q_s, q_r, z_s, z_r, e_s, e_r,
):
    bs, r1, s1, r2 = (b0, b1, b2), (r10, r11, r12), (s10, s11, s12), (r20, r21, r22)
    halves, nears = (h0, h1, h2), (n0, n1, n2)
    s2, r3, k2 = (s20, s21, s22), (r30, r31, r32), (k20, k21, k22)
    me = lax.axis_index("seq")
    c = lax.rem(me, 2)
    y = lax.rem(me // 2, 4)
    z = lax.rem(me // 8, 4)
    x = me // 32
    chip = me // 2
    mate = me + 1 - 2 * c
    coords, strides = (x, z, y), (32, 8, 2)

    def along(axis, k):
        there = lax.rem(coords[axis] + k, 4)
        return there, me + (there - coords[axis]) * strides[axis]

    def rcopy(src, dst, send, recv, dev):
        return pltpu.make_async_remote_copy(
            src_ref=src, dst_ref=dst, send_sem=send, recv_sem=recv,
            device_id=(dev,), device_id_type=MESH,
        )

    inputs = [
        pltpu.make_async_copy(src, dst, in_sem.at[i])
        for i, (src, dst) in enumerate(
            ((srow_in, srow), (tok_in, tok), (gout_in, gout), (rplace_in, rplace),
             (stamps_in, stamps), (relb_in, relb))
        )
    ]
    for load in inputs:
        load.start()
    barrier = pltpu.get_barrier_semaphore()

    pl.semaphore_signal(barrier, inc=1, device_id=(mate,), device_id_type=MESH)
    for axis in range(3):
        for k in range(1, 4):
            pl.semaphore_signal(
                barrier, inc=1, device_id=(along(axis, k)[1] + mate - me,), device_id_type=MESH
            )

    @pl.loop(1, 64)
    def _(k):
        pl.semaphore_signal(
            barrier, inc=1, device_id=(lax.rem(chip + k, 64) * 2 + c,), device_id_type=MESH
        )

    half = pl.multiple_of(c * 512, 512)
    loads = [
        pltpu.make_async_copy(w_in.at[:, pl.ds(f * 1024 + half, 512)], wi.at[f], wsem.at[f])
        for f in range(4)
    ]
    loads.append(pltpu.make_async_copy(w_out.at[:, pl.ds(half, 512)], wo, wsem.at[4]))

    rows = lax.broadcasted_iota(jnp.int32, (128, 128), 0)
    lanes = lax.broadcasted_iota(jnp.int32, (128, 128), 1)
    eye = rows == lanes

    def to_column(row):
        return jnp.sum(jnp.where(eye, row, 0.0), axis=1, keepdims=True)

    def to_row(column):
        return jnp.sum(jnp.where(eye, column, 0.0), axis=0, keepdims=True)

    for load in inputs:
        load.wait()
    order = ((rows & 63) << 1) + (rows >> 6)
    wanted = jnp.sum(
        jnp.where(lanes == order, srow[...].astype(F32), 0.0), axis=1, keepdims=True
    )
    pick = jnp.where(wanted == lanes.astype(F32), 1.0, 0.0).astype(BF16)

    def fold(value, kind, start=0):
        for o in range(2):
            for j in range(8):
                sf[kind, pl.ds(o * 8 + j, 64, stride=16), :] = value(
                    slice(64 * o, 64 * o + 64), slice(128 * j, 128 * j + 128)
                )
        sa[:, 16 * kind : 16 * kind + 16] = sf[kind].reshape(64, 16, 128).astype(BF16)

    def unfolded(ref, o):
        return jnp.concatenate(
            [ref[pl.ds(o * 8 + j, 64, stride=16), :] for j in range(8)], axis=1
        ).astype(BF16)

    picked = dot(pick, tok[...])
    fold(lambda at, cols: picked[at, cols], 0)

    pl.semaphore_wait(barrier, 73)

    def peer(i, j):
        there = lax.rem(x + i, 4) * 16 + lax.rem(z * 4 + y + j, 16)
        return there, there * 2 + c

    def scatter(rows, dst, sends, recvs):
        @pl.loop(0, 16)
        def _(j):
            for i in range(4):
                there, dev = peer(i, j)

                def go():
                    src = sa.at[there, rows]
                    rcopy(src, dst.at[chip], sends.at[i], recvs.at[i], dev).start()

                if i == 0:
                    pl.when(j > 0)(go)
                else:
                    go()

    def scattered(dst, sends, recvs, i):
        ref = dst.at[pl.ds(lax.rem(x + 4 - i, 4) * 16, 16 if i else 15)]
        return rcopy(ref, ref, sends.at[i], recvs.at[i], mate)

    def outward(kind, i):
        at = pl.ds(4 * kind, 4)
        return scattered(rg.at[kind, c], a_s.at[at], a_r.at[at], i)

    def leave(kind):
        rows, at = pl.ds(16 * kind, 16), pl.ds(4 * kind, 4)
        scatter(rows, rg.at[kind, c], a_s.at[at], a_r.at[at])
        rg[kind, c, chip] = sa[chip, rows]

    leave(0)
    picked_g = dot(pick, gout[...])
    fold(lambda at, cols: picked_g[at, cols], 1)
    leave(1)
    for load in loads:
        load.start()

    m = rplace[...]
    place = (m & 1) * 64 + (m >> 1)
    lands = place == rows
    slot = to_row(jnp.sum(jnp.where(lands, lanes.astype(F32), 0.0), axis=1, keepdims=True))
    when = to_row(jnp.sum(jnp.where(lands, stamps[...].astype(F32), 0.0), axis=1, keepdims=True))
    alive = slot < (live[0] + first[0] * 128).astype(F32)
    sub = lax.broadcasted_iota(jnp.int32, (8, 128), 0)
    meta[c] = jnp.where(
        sub == 0,
        jnp.where(alive, slot, 1e6),
        jnp.where(sub == 1, jnp.where(alive, slot, -1.0), when),
    )
    meta_copy = rcopy(meta.at[c], meta.at[c], m_s, m_r, mate)
    meta_copy.start()

    def wait_meta():
        rcopy(meta.at[1 - c], meta.at[1 - c], m_s, m_r, mate).wait_recv()

    wait_meta()
    for o in range(2):
        keys, asks, times = meta[o, 0:1], to_column(meta[o, 1:2]), meta[o, 2:3]
        mask[o] = jnp.where(keys <= asks, 1.0, 0.0)
        spread = to_column(times) - times

        @pl.loop(0, 4)
        def _(h, o=o, spread=spread):
            value = jnp.full((128, 128), relb[4 * c + h, 0], F32)
            for k in range(15):
                value = jnp.where(spread >= float(2**k), relb[4 * c + h, k + 1], value)
            bias[4 * o + h] = value

    def forward(kind, cs, i):
        at = pl.ds(lax.rem(x + 4 - i, 4) * 16, 16)
        ref = rg.at[kind, cs, at]
        return rcopy(ref, ref, c_s.at[4 * kind + i], c_r.at[4 * kind + i], mate)

    def widen(kind, cs, i):
        at = lax.rem(x + 4 - i, 4)
        wide = rg[kind, cs, pl.ds(at * 16, 16)].astype(F32).reshape(256, 128)
        rf[kind, cs, pl.ds(pl.multiple_of(at * 256, 256), 256)] = wide

    def arrive(kind):
        for i in (0, 1, 3, 2):
            outward(kind, i).wait_recv()
            forward(kind, c, i).start()
            widen(kind, c, i)

    def complete(kind, into):
        for i in (0, 1, 3, 2):
            forward(kind, 1 - c, i).wait_recv()
            widen(kind, 1 - c, i)
        for o in range(2):
            for cs in range(2):
                here = slice(128 * o + 64 * cs, 128 * o + 64 * cs + 64)
                into[here] = unfolded(rf.at[kind, cs], o)

    arrive(0)
    complete(0, xv)

    def pair(o, e):
        here = coords[o]
        turn = 1 - 2 * lax.rem(here + e + c, 2)
        one, two = lax.rem(here + 4 + turn, 4), lax.rem(here + 4 - turn, 4)
        to_one, to_two = (me + (n - here) * strides[o] for n in (one, two))
        return here, lax.rem(here + 2, 4), one, two, to_one, to_two

    def quarter(ref, o, q):
        return ref.at[(slice(None),) * o + (q,)]

    def early(o, e):
        _, across, one, _, dev, _ = pair(o, e)
        i = (o * 2 + e) * 2
        return [
            rcopy(quarter(xt, o, q), xn.at[o, e, n], e_s.at[i + n], e_r.at[i + n], dev)
            for n, q in ((1, across), (0, one))
        ]

    xt[...] = xv[...].T.reshape(4, 4, 4, 16, 256)
    for e in range(2):
        for o in range(3):
            for copy in early(o, e):
                copy.start()
    for load in loads:
        load.wait()

    def project(f):
        pre = dot(xv[...], wi[f])
        sig = jax.nn.sigmoid(pre)
        act[f] = (pre * sig).astype(BF16)
        slp[f] = sig * (1.0 + pre * (1.0 - sig))

    project(1)
    project(2)
    arrive(1)
    project(3)
    project(0)
    heads = [(o, h) for o in range(2) for h in range(4)]
    scale = 128**-0.5
    for o, h in heads:
        here = (slice(128 * o, 128 * o + 128), slice(128 * h, 128 * h + 128))
        v, q, k = (act[(f,) + here] for f in (1, 2, 3))
        logits = dot(q, k, ((1,), (1,))) * scale + bias[4 * o + h]
        sig = jax.nn.sigmoid(logits)
        allowed = mask[o] > 0.5
        w = jnp.where(allowed, logits * sig, 0.0).astype(BF16)
        pw[4 * o + h] = w
        ps[4 * o + h] = jnp.where(allowed, sig * (1.0 + logits * (1.0 - sig)), 0.0)
        mix[here] = dot(w, v)

    complete(1, gv)
    gg[...] = dot(gv[...], wo[...])

    gn = gg[...] * act[0].astype(F32)
    mixed = mix[...]
    total = jnp.sum(mixed, axis=1, keepdims=True)
    centre = mixed - total * (1.0 / 512)
    square = jnp.sum(centre * centre, axis=1, keepdims=True)
    gsum = jnp.sum(gn, axis=1, keepdims=True)
    gdot = jnp.sum(gn * centre, axis=1, keepdims=True)
    col = lax.broadcasted_iota(jnp.int32, (256, 128), 1)
    stat[c] = jnp.where(
        col == 0, total, jnp.where(col == 1, square, jnp.where(col == 2, gsum, gdot))
    )
    stat_copy = rcopy(stat.at[c], stat.at[c], t_s, t_r, mate)
    stat_copy.start()
    gt[...] = gv[...].T.reshape(4, 4, 4, 16, 256)
    rcopy(stat.at[1 - c], stat.at[1 - c], t_s, t_r, mate).wait_recv()
    theirs = stat[1 - c]
    total2, square2, gsum2, gdot2 = (theirs[:, i : i + 1] for i in range(4))
    mean = (total + total2) * (1.0 / 1024)
    off, off2 = total * (1.0 / 512) - mean, total2 * (1.0 / 512) - mean
    var = (square + square2 + 512.0 * (off * off + off2 * off2)) * (1.0 / 1024)
    inv_std = lax.rsqrt(var + EPS)
    mean_gn = (gsum + gsum2) * (1.0 / 1024)
    mean_gnn = (gdot + off * gsum + gdot2 + off2 * gsum2) * inv_std * (1.0 / 1024)
    normed = (mix[...] - mean) * inv_std
    upper = act[0].astype(F32)
    ga[...] = (normed * upper).astype(BF16)
    ggv = gg[...]
    gm[...] = (inv_std * (ggv * upper - mean_gn - normed * mean_gnn)).astype(BF16)
    gp[0] = ((ggv * normed).astype(BF16).astype(F32) * slp[0]).astype(BF16)

    def product(block, left, right):
        @pl.loop(0, 4, unroll=True)
        def _(i):
            tile = dot(left[i].reshape(256, 256), right).astype(BF16)
            seen = [0, 0, 0]
            for j in range(4):
                o = ORDERS[block][j]
                at = slots(block, o)[0] + seen[o]
                seen[o] += 1
                part4 = tile[:, 128 * j : 128 * j + 128].reshape(4, 4, 16, 128)
                if o == 0:
                    bs[0][at, i] = part4
                elif o == 1:
                    bs[1][at, :, :, i] = part4
                else:
                    for k in range(4):
                        bs[2][at, :, i, k] = part4[k]

    def tiles(block):
        return [(o, t) for o in range(3) for t in range(slots(block, o)[0], sum(slots(block, o)))]

    def near(step, o, t):
        _, across, one, two, dev, dev2 = pair(o, t % 2)
        i = (sum(COUNT[:o]) + t) * 3
        sems = [(p1_s.at[i + n], p1_r.at[i + n]) for n in range(3)]
        if step == 0:
            return [
                rcopy(bs[o].at[t, q], r1[o].at[t, n], *sems[n], dev)
                for n, q in ((1, across), (0, one))
            ]
        return two, rcopy(halves[o].at[t], nears[o].at[t], *sems[2], dev2)

    def column(block, o, t):
        return [j for j in range(4) if ORDERS[block][j] == o][t - slots(block, o)[0]]

    def swap(block, o, t):
        i = sum(COUNT[:o]) + t
        mine = gp.at[block - 1, :, pl.ds(128 * column(block, o, t), 128)]
        theirs = yn.at[i]
        return mine, theirs, rcopy(mine, theirs, p1_s.at[3 * i], p1_r.at[3 * i], pair(o, t % 2)[4])

    def near_send(block, columns=(0, 1, 2, 3)):
        for o, t in tiles(block):
            if column(block, o, t) in columns:
                for copy in near(0, o, t) if block < 2 else [swap(block, o, t)[2]]:
                    copy.start()

    came = set()

    def near_pass(block):
        for o, t in tiles(block):
            e = t % 2
            here, _, _, two, _, _ = pair(o, e)
            copy = near(1, o, t)[1]
            if block < 2:
                near(0, o, t)[0].wait_recv()
                halves[o][t] = (bs[o][t, two].astype(F32) + r1[o][t, 1].astype(F32)).astype(BF16)
                copy.start()
                continue
            if (o, e) not in came:
                came.add((o, e))
                for arrival in early(o, e):
                    arrival.wait_recv()
            mine, theirs, swapped = swap(block, o, t)
            swapped.wait_recv()
            for n, q in ((1, two), (0, here)):
                left = quarter(xt, o, q)[...].reshape(256, 256)
                value = dot(left, mine[...]) + dot(xn[o, e, n].reshape(256, 256), theirs[...])
                value = value.astype(BF16).reshape(4, 4, 16, 128)
                into = halves[o].at[t] if n else bs[o].at[t, here]
                if o == 1:
                    for k in range(4):
                        into[:, k] = value[k]
                else:
                    into[...] = value
                if n:
                    copy.start()

    def near_add(block):
        for o, t in tiles(block):
            near(1, o, t)[1].wait_recv()
            value = bs[o][t, coords[o]].astype(F32) + nears[o][t].astype(F32)
            if block < 2:
                near(0, o, t)[1].wait_recv()
                value = value + r1[o][t, 0].astype(F32)
            s1[o][t] = value.astype(BF16)

    def hop(block, o, k):
        there, dev = along((o + 1) % 3, k)
        start, count = slots(block, o)
        at = pl.ds(start, count)
        i = (block * 3 + o) * 3 + k - 1
        return rcopy(s1[o].at[at, there], r2[o].at[k - 1, at], p2_s.at[i], p2_r.at[i], dev)

    def pack():
        for o in range(3):
            for core in range(2):
                for n in range(PAIRS[o]):
                    rows8 = [
                        s2[o][min(i, COUNT[o] - 1), :, 8 * core : 8 * core + 8]
                        for i in (2 * n, 2 * n + 1)
                    ]
                    k2[o][:, core, n] = jnp.concatenate(rows8, axis=1).astype(BF16)

    def last(o, k, rel, sending=True):
        there, dev = along((o + 2) % 3, k)
        i = (o * 4 + k) * 2 + rel
        mine, far = (c, 1 - c) if rel else (c, c)
        dst = r3[o].at[mine if sending else far, k]
        return rcopy(
            k2[o].at[there, far], dst, p3_s.at[i], p3_r.at[i], dev + mate - me if rel else dev
        )

    lasts = [(o, k, rel) for k in (2, 1, 3, 0) for o in range(3) for rel in range(2) if k or rel]

    def far_send(block):
        near_add(block)
        for k in (2, 1, 3):
            for o in range(3):
                hop(block, o, k).start()

    def far_add(block):
        for o in range(3):
            for k in range(1, 4):
                hop(block, o, k).wait_recv()
            start, count = slots(block, o)
            at = slice(start, start + count)
            value = s1[o][at, coords[(o + 1) % 3]].astype(F32)
            for k in range(3):
                value = value + r2[o][k, at].astype(F32)
            s2[o][at] = value

    product(0, gt, ga[...])
    near_send(0)
    product(1, xt, gp[0])
    near_send(1)
    part[0] = dot(ga[...], wo[...], ((1,), (1,))).reshape(2, 2, 64, 1024)

    def across(kind):
        return rcopy(part.at[kind, :, 1 - c], rpart.at[kind], q_s.at[kind], q_r.at[kind], mate)

    def home(kind):
        across(kind).wait_recv()
        mine = pl.multiple_of(64 * c, 64)
        total = [part[kind, o, c] + rpart[kind, o] for o in range(2)]
        if kind:
            for o in range(2):
                total[o] = total[o] + gv[pl.ds(128 * o + mine, 64), :].astype(F32)
        for i in range(4):
            outward(kind, i).wait_send()
        fold(lambda at, cols: total[at.start // 64][:, cols], kind)

    across(0).start()

    for h, o in [(h, o) for h in range(4) for o in range(2)]:
        here = (slice(128 * o, 128 * o + 128), slice(128 * h, 128 * h + 128))
        v, q, k = (act[(f,) + here] for f in (1, 2, 3))
        gmh, w = gm[here], pw[4 * o + h]
        gl = (dot(gmh, v, ((1,), (1,))) * ps[4 * o + h]).astype(BF16)
        grads = (
            dot(w, gmh, ((0,), (0,))),
            dot(gl, k) * scale,
            dot(gl, q, ((0,), (0,))) * scale,
        )
        for f in (1, 2, 3):
            gp[(f,) + here] = (
                grads[f - 1].astype(BF16).astype(F32) * slp[(f,) + here]
            ).astype(BF16)
        if o == 1 and h % 2 == 1:
            for block in range(2, 5):
                near_send(block, (h - 1, h))
    near_pass(0)
    near_pass(1)
    back = dot(gp[0], wi[0], ((1,), (1,)))
    for f in range(1, 4):
        back = back + dot(gp[f], wi[f], ((1,), (1,)))
    part[1] = back.reshape(2, 2, 64, 1024)
    across(1).start()
    near_pass(2)
    near_pass(3)
    near_pass(4)
    far_send(0)
    far_send(1)
    home(0)
    home(1)
    for block in range(2, 5):
        far_send(block)
    scatter(pl.ds(0, 32), rz, z_s, z_r)
    rz[chip] = sa[chip]
    for block in range(5):
        far_add(block)
    pack()
    for step in lasts:
        last(*step).start()
    unpick = jnp.where(to_row(wanted) == rows.astype(F32), 1.0, 0.0).astype(BF16)

    for i in range(4):
        scattered(rz, z_s, z_r, i).wait_recv()

    def returned(kind):
        sf[kind] = rz[:, 16 * kind : 16 * kind + 16].astype(F32).reshape(1024, 128)
        return dot(
            unpick, jnp.concatenate([unfolded(sf.at[kind], o) for o in range(2)], axis=0)
        )

    out[...] = (tok[...].astype(F32) + returned(0)).astype(BF16)
    gx[...] = returned(1).astype(BF16)

    for o, k, rel in lasts:
        last(o, k, rel, False).wait_recv()
    other = pl.multiple_of(512 - half, 512)
    for o in range(3):
        here = coords[(o + 2) % 3]
        for side, base in ((c, half), (1 - c, other)):
            first_term = k2[o][here, c] if base is half else r3[o][side, 0]
            value = first_term.astype(F32)
            for k in range(1, 4):
                value = value + r3[o][side, k].astype(F32)
            for block in range(5):
                for t in range(slots(block, o)[0], sum(slots(block, o))):
                    tile = value[t // 2, 8 * (t % 2) : 8 * (t % 2) + 8]
                    at = 128 * column(block, o, t)
                    if block == 0:
                        gw2[:, pl.ds(base + at, 128)] = tile
                    else:
                        gw1[:, pl.ds((block - 1) * 1024 + base + at, 128)] = tile

    for i in range(4):
        scattered(rz, z_s, z_r, i).wait_send()
        for kind in range(2):
            forward(kind, c, i).wait_send()
    for kind in range(2):
        across(kind).wait_send()
    meta_copy.wait_send()
    stat_copy.wait_send()
    for step in lasts:
        last(*step).wait_send()
    for k in range(1, 4):
        for o in range(3):
            for block in range(5):
                hop(block, o, k).wait_send()
    for block in range(5):
        for o, t in tiles(block):
            near(1, o, t)[1].wait_send()
            for copy in near(0, o, t) if block < 2 else [swap(block, o, t)[2]]:
                copy.wait_send()
    for e in range(2):
        for o in range(3):
            for copy in early(o, e):
                copy.wait_send()


def hand_over(*refs):
    for i in range(4):
        refs[4 + i][...] = refs[i][...]


def body(
    tokens, grad_out, w_in, w_out, rel_bias, send_rows, recv_place, block_first, user_rows, stamps
):
    vmem, smem = pl.BlockSpec(memory_space=pltpu.VMEM), pl.BlockSpec(memory_space=pltpu.SMEM)
    hbm = pl.BlockSpec(memory_space=pl.ANY)
    dma = pltpu.SemaphoreType.DMA

    def v(shape, kind=BF16):
        return pltpu.VMEM(shape, kind)

    scratch = [
        v((128, 1024)), v((128, 1024)), pltpu.SMEM((8, 16), F32), v((1, 128), jnp.int32),
        v((1, 128), jnp.int32), v((1, 128), jnp.int32),
        v((4, 1024, 512)), v((1024, 512)), v((2, 1024, 128), F32), v((64, 32, 128)),
        v((2, 2, 64, 16, 128)), v((2, 2, 1024, 128), F32), v((2, 8, 128), F32),
        v((8, 128, 128), F32), v((2, 128, 128), F32), v((256, 1024)), v((256, 1024)),
        v((4, 4, 4, 16, 256)), v((4, 4, 4, 16, 256)), v((4, 256, 512)), v((4, 256, 512), F32),
        v((8, 128, 128)), v((8, 128, 128), F32), v((256, 512), F32), v((256, 512), F32),
        v((2, 256, 128), F32), v((256, 512)), v((256, 512)), v((4, 256, 512)),
    ]
    scratch += [v((n, 4, 4, 4, 16, 128)) for n in COUNT]
    scratch += [v((n, 2, 4, 4, 16, 128)) for n in COUNT]
    scratch += [v((n, 4, 4, 16, 128)) for n in COUNT]
    scratch += [v((n, 4, 4, 16, 128)) for n in COUNT]
    scratch += [v((n, 4, 4, 16, 128)) for n in COUNT]
    scratch += [v((3, n, 4, 16, 128)) for n in COUNT]
    scratch += [v((n, 4, 16, 128), F32) for n in COUNT]
    scratch += [v((2, 4, n, 16, 128)) for n in PAIRS]
    scratch += [v((4, 2, n, 16, 128)) for n in PAIRS]
    scratch += [
        v((2, 2, 2, 64, 1024), F32),
        v((2, 2, 64, 1024), F32), v((64, 32, 128)), v((3, 2, 2, 4, 4, 16, 256)),
        v((20, 256, 128)),
    ]
    scratch += [dma((6,)), dma((5,)), dma((8,)), dma((8,)), dma((8,)), dma((8,))]
    scratch += [dma, dma, dma, dma, dma((60,)), dma((60,)), dma((45,)), dma((45,))]
    scratch += [dma((24,)), dma((24,)), dma((2,)), dma((2,)), dma((4,)), dma((4,))]
    scratch += [dma((12,)), dma((12,))]
    results = pl.pallas_call(
            kernel,
            out_shape=(
                jax.ShapeDtypeStruct((128, 1024), BF16),
                jax.ShapeDtypeStruct((128, 1024), BF16),
                jax.ShapeDtypeStruct((8, 4096), F32),
                jax.ShapeDtypeStruct((8, 1024), F32),
            ),
            in_specs=[hbm] * 7 + [smem, smem, hbm],
            out_specs=(vmem, vmem, vmem, vmem),
            scratch_shapes=scratch,
            compiler_params=pltpu.CompilerParams(
                collective_id=0, has_side_effects=True, vmem_limit_bytes=56 * 2**20
            ),
        )(
            tokens, grad_out, w_in, w_out, rel_bias, send_rows, recv_place, block_first,
            user_rows, stamps.reshape(1, 128),
        )
    return pl.pallas_call(
        hand_over,
        out_shape=tuple(jax.ShapeDtypeStruct(r.shape, r.dtype) for r in results),
        in_specs=[vmem] * 4,
        out_specs=(vmem,) * 4,
    )(*results)


def solution(mesh):
    placed = (
        P("seq", None), P("seq", None), P(), P(), P(), P("seq", None), P("seq", None),
        P("seq"), P("seq"), P("seq"),
    )
    return jax.shard_map(
        body,
        mesh=mesh,
        in_specs=placed,
        out_specs=(P("seq", None), P("seq", None), P("seq", None), P("seq", None)),
        check_vma=False,
    )
```

```python
import functools

import jax
import jax.numpy as jnp
from jax import lax
from jax.experimental import pallas as pl
from jax.experimental.pallas import tpu as pltpu
from jax.sharding import PartitionSpec as P

EPS = 1e-05
F32, BF16 = jnp.float32, jnp.bfloat16
MESH = pl.DeviceIdType.MESH
ORDERS = ((0, 0, 1, 2), (0, 1, 1, 2), (0, 1, 2, 2), (0, 0, 1, 2), (0, 1, 1, 2))
COUNT = tuple(sum(row.count(o) for row in ORDERS) for o in range(3))
PAIRS = tuple((n + 1) // 2 for n in COUNT)


def slots(block, order):
    start = sum(row.count(order) for row in ORDERS[:block])
    return start, ORDERS[block].count(order)


def dot(a, b, dims=((1,), (0,))):
    return lax.dot_general(a, b, (dims, ((), ())), preferred_element_type=F32)


def kernel(
    tok_in, gout_in, w_in, w_out, relb_in, srow_in, rplace_in, first, live, stamps_in,
    out, gx, gw1, gw2,
    tok, gout, relb, srow, rplace, stamps, wi, wo, sf, sa, rg, rf, meta, bias, mask, xv, gv, xt, gt, act, slp, pw, ps, mix, gg,
    stat, ga, gm, gp, b0, b1, b2, r10, r11, r12, h0, h1, h2, n0, n1, n2, s10, s11, s12, r20, r21, r22, s20, s21, s22,
    r30, r31, r32, k20, k21, k22, part, rpart, rz, xn, yn,
    in_sem, wsem, a_s, a_r, c_s, c_r, m_s, m_r, t_s, t_r, p1_s, p1_r, p2_s, p2_r, p3_s, p3_r,
    q_s, q_r, z_s, z_r, e_s, e_r,
):
    bs, r1, s1, r2 = (b0, b1, b2), (r10, r11, r12), (s10, s11, s12), (r20, r21, r22)
    halves, nears = (h0, h1, h2), (n0, n1, n2)
    s2, r3, k2 = (s20, s21, s22), (r30, r31, r32), (k20, k21, k22)
    me = lax.axis_index("seq")
    c = lax.rem(me, 2)
    y = lax.rem(me // 2, 4)
    z = lax.rem(me // 8, 4)
    x = me // 32
    chip = me // 2
    mate = me + 1 - 2 * c
    coords, strides = (x, z, y), (32, 8, 2)

    def along(axis, k):
        there = lax.rem(coords[axis] + k, 4)
        return there, me + (there - coords[axis]) * strides[axis]

    def rcopy(src, dst, send, recv, dev):
        return pltpu.make_async_remote_copy(
            src_ref=src, dst_ref=dst, send_sem=send, recv_sem=recv,
            device_id=(dev,), device_id_type=MESH,
        )

    inputs = [
        pltpu.make_async_copy(src, dst, in_sem.at[i])
        for i, (src, dst) in enumerate(
            ((srow_in, srow), (tok_in, tok), (gout_in, gout), (rplace_in, rplace),
             (stamps_in, stamps), (relb_in, relb))
        )
    ]
    for load in inputs:
        load.start()
    barrier = pltpu.get_barrier_semaphore()

    pl.semaphore_signal(barrier, inc=1, device_id=(mate,), device_id_type=MESH)
    for axis in range(3):
        for k in range(1, 4):
            pl.semaphore_signal(
                barrier, inc=1, device_id=(along(axis, k)[1] + mate - me,), device_id_type=MESH
            )

    @pl.loop(1, 64)
    def _(k):
        pl.semaphore_signal(
            barrier, inc=1, device_id=(lax.rem(chip + k, 64) * 2 + c,), device_id_type=MESH
        )

    half = pl.multiple_of(c * 512, 512)
    loads = [
        pltpu.make_async_copy(w_in.at[:, pl.ds(f * 1024 + half, 512)], wi.at[f], wsem.at[f])
        for f in range(4)
    ]
    loads.append(pltpu.make_async_copy(w_out.at[:, pl.ds(half, 512)], wo, wsem.at[4]))

    rows = lax.broadcasted_iota(jnp.int32, (128, 128), 0)
    lanes = lax.broadcasted_iota(jnp.int32, (128, 128), 1)
    eye = rows == lanes

    def to_column(row):
        return jnp.sum(jnp.where(eye, row, 0.0), axis=1, keepdims=True)

    def to_row(column):
        return jnp.sum(jnp.where(eye, column, 0.0), axis=0, keepdims=True)

    for load in inputs:
        load.wait()
    order = ((rows & 63) << 1) + (rows >> 6)
    wanted = jnp.sum(
        jnp.where(lanes == order, srow[...].astype(F32), 0.0), axis=1, keepdims=True
    )
    pick = jnp.where(wanted == lanes.astype(F32), 1.0, 0.0).astype(BF16)

    def fold(value, kind, start=0):
        for o in range(2):
            for j in range(8):
                sf[kind, pl.ds(o * 8 + j, 64, stride=16), :] = value(
                    slice(64 * o, 64 * o + 64), slice(128 * j, 128 * j + 128)
                )
        sa[:, 16 * kind : 16 * kind + 16] = sf[kind].reshape(64, 16, 128).astype(BF16)

    def unfolded(ref, o):
        return jnp.concatenate(
            [ref[pl.ds(o * 8 + j, 64, stride=16), :] for j in range(8)], axis=1
        ).astype(BF16)

    picked = dot(pick, tok[...])
    fold(lambda at, cols: picked[at, cols], 0)

    pl.semaphore_wait(barrier, 73)

    def peer(i, j):
        there = lax.rem(x + i, 4) * 16 + lax.rem(z * 4 + y + j, 16)
        return there, there * 2 + c

    def scatter(rows, dst, sends, recvs):
        @pl.loop(0, 16)
        def _(j):
            for i in range(4):
                there, dev = peer(i, j)

                def go():
                    src = sa.at[there, rows]
                    rcopy(src, dst.at[chip], sends.at[i], recvs.at[i], dev).start()

                if i == 0:
                    pl.when(j > 0)(go)
                else:
                    go()

    def scattered(dst, sends, recvs, i):
        ref = dst.at[pl.ds(lax.rem(x + 4 - i, 4) * 16, 16 if i else 15)]
        return rcopy(ref, ref, sends.at[i], recvs.at[i], mate)

    def outward(kind, i):
        at = pl.ds(4 * kind, 4)
        return scattered(rg.at[kind, c], a_s.at[at], a_r.at[at], i)

    def leave(kind):
        rows, at = pl.ds(16 * kind, 16), pl.ds(4 * kind, 4)
        scatter(rows, rg.at[kind, c], a_s.at[at], a_r.at[at])
        rg[kind, c, chip] = sa[chip, rows]

    leave(0)
    picked_g = dot(pick, gout[...])
    fold(lambda at, cols: picked_g[at, cols], 1)
    leave(1)
    for load in loads:
        load.start()

    m = rplace[...]
    place = (m & 1) * 64 + (m >> 1)
    lands = place == rows
    slot = to_row(jnp.sum(jnp.where(lands, lanes.astype(F32), 0.0), axis=1, keepdims=True))
    when = to_row(jnp.sum(jnp.where(lands, stamps[...].astype(F32), 0.0), axis=1, keepdims=True))
    alive = slot < (live[0] + first[0] * 128).astype(F32)
    sub = lax.broadcasted_iota(jnp.int32, (8, 128), 0)
    meta[c] = jnp.where(
        sub == 0,
        jnp.where(alive, slot, 1e6),
        jnp.where(sub == 1, jnp.where(alive, slot, -1.0), when),
    )
    meta_copy = rcopy(meta.at[c], meta.at[c], m_s, m_r, mate)
    meta_copy.start()

    def wait_meta():
        rcopy(meta.at[1 - c], meta.at[1 - c], m_s, m_r, mate).wait_recv()

    wait_meta()
    for o in range(2):
        keys, asks, times = meta[o, 0:1], to_column(meta[o, 1:2]), meta[o, 2:3]
        mask[o] = jnp.where(keys <= asks, 1.0, 0.0)
        spread = to_column(times) - times

        @pl.loop(0, 4)
        def _(h, o=o, spread=spread):
            value = jnp.full((128, 128), relb[4 * c + h, 0], F32)
            for k in range(15):
                value = jnp.where(spread >= float(2**k), relb[4 * c + h, k + 1], value)
            bias[4 * o + h] = value

    def forward(kind, cs, i):
        at = pl.ds(lax.rem(x + 4 - i, 4) * 16, 16)
        ref = rg.at[kind, cs, at]
        return rcopy(ref, ref, c_s.at[4 * kind + i], c_r.at[4 * kind + i], mate)

    def widen(kind, cs, i):
        at = lax.rem(x + 4 - i, 4)
        wide = rg[kind, cs, pl.ds(at * 16, 16)].astype(F32).reshape(256, 128)
        rf[kind, cs, pl.ds(pl.multiple_of(at * 256, 256), 256)] = wide

    def arrive(kind):
        for i in (0, 1, 3, 2):
            outward(kind, i).wait_recv()
            forward(kind, c, i).start()
            widen(kind, c, i)

    def complete(kind, into):
        for i in (0, 1, 3, 2):
            forward(kind, 1 - c, i).wait_recv()
            widen(kind, 1 - c, i)
        for o in range(2):
            for cs in range(2):
                here = slice(128 * o + 64 * cs, 128 * o + 64 * cs + 64)
                into[here] = unfolded(rf.at[kind, cs], o)

    arrive(0)
    complete(0, xv)

    def pair(o, e):
        here = coords[o]
        turn = 1 - 2 * lax.rem(here + e + c, 2)
        one, two = lax.rem(here + 4 + turn, 4), lax.rem(here + 4 - turn, 4)
        to_one, to_two = (me + (n - here) * strides[o] for n in (one, two))
        return here, lax.rem(here + 2, 4), one, two, to_one, to_two

    def quarter(ref, o, q):
        return ref.at[(slice(None),) * o + (q,)]

    def early(o, e):
        _, across, one, _, dev, _ = pair(o, e)
        i = (o * 2 + e) * 2
        return [
            rcopy(quarter(xt, o, q), xn.at[o, e, n], e_s.at[i + n], e_r.at[i + n], dev)
            for n, q in ((1, across), (0, one))
        ]

    xt[...] = xv[...].T.reshape(4, 4, 4, 16, 256)
    for e in range(2):
        for o in range(3):
            for copy in early(o, e):
                copy.start()
    for load in loads:
        load.wait()

    def project(f):
        pre = dot(xv[...], wi[f])
        sig = jax.nn.sigmoid(pre)
        act[f] = (pre * sig).astype(BF16)
        slp[f] = sig * (1.0 + pre * (1.0 - sig))

    project(1)
    project(2)
    arrive(1)
    project(3)
    project(0)
    heads = [(o, h) for o in range(2) for h in range(4)]
    scale = 128**-0.5
    for o, h in heads:
        here = (slice(128 * o, 128 * o + 128), slice(128 * h, 128 * h + 128))
        v, q, k = (act[(f,) + here] for f in (1, 2, 3))
        logits = dot(q, k, ((1,), (1,))) * scale + bias[4 * o + h]
        sig = jax.nn.sigmoid(logits)
        allowed = mask[o] > 0.5
        w = jnp.where(allowed, logits * sig, 0.0).astype(BF16)
        pw[4 * o + h] = w
        ps[4 * o + h] = jnp.where(allowed, sig * (1.0 + logits * (1.0 - sig)), 0.0)
        mix[here] = dot(w, v)

    complete(1, gv)
    gg[...] = dot(gv[...], wo[...])

    gn = gg[...] * act[0].astype(F32)
    mixed = mix[...]
    total = jnp.sum(mixed, axis=1, keepdims=True)
    centre = mixed - total * (1.0 / 512)
    square = jnp.sum(centre * centre, axis=1, keepdims=True)
    gsum = jnp.sum(gn, axis=1, keepdims=True)
    gdot = jnp.sum(gn * centre, axis=1, keepdims=True)
    col = lax.broadcasted_iota(jnp.int32, (256, 128), 1)
    stat[c] = jnp.where(
        col == 0, total, jnp.where(col == 1, square, jnp.where(col == 2, gsum, gdot))
    )
    stat_copy = rcopy(stat.at[c], stat.at[c], t_s, t_r, mate)
    stat_copy.start()
    gt[...] = gv[...].T.reshape(4, 4, 4, 16, 256)
    rcopy(stat.at[1 - c], stat.at[1 - c], t_s, t_r, mate).wait_recv()
    theirs = stat[1 - c]
    total2, square2, gsum2, gdot2 = (theirs[:, i : i + 1] for i in range(4))
    mean = (total + total2) * (1.0 / 1024)
    off, off2 = total * (1.0 / 512) - mean, total2 * (1.0 / 512) - mean
    var = (square + square2 + 512.0 * (off * off + off2 * off2)) * (1.0 / 1024)
    inv_std = lax.rsqrt(var + EPS)
    mean_gn = (gsum + gsum2) * (1.0 / 1024)
    mean_gnn = (gdot + off * gsum + gdot2 + off2 * gsum2) * inv_std * (1.0 / 1024)
    normed = (mix[...] - mean) * inv_std
    upper = act[0].astype(F32)
    ga[...] = (normed * upper).astype(BF16)
    ggv = gg[...]
    gm[...] = (inv_std * (ggv * upper - mean_gn - normed * mean_gnn)).astype(BF16)
    gp[0] = ((ggv * normed).astype(BF16).astype(F32) * slp[0]).astype(BF16)

    def product(block, left, right):
        @pl.loop(0, 4, unroll=True)
        def _(i):
            tile = dot(left[i].reshape(256, 256), right).astype(BF16)
            seen = [0, 0, 0]
            for j in range(4):
                o = ORDERS[block][j]
                at = slots(block, o)[0] + seen[o]
                seen[o] += 1
                part4 = tile[:, 128 * j : 128 * j + 128].reshape(4, 4, 16, 128)
                if o == 0:
                    bs[0][at, i] = part4
                elif o == 1:
                    bs[1][at, :, :, i] = part4
                else:
                    for k in range(4):
                        bs[2][at, :, i, k] = part4[k]

    def tiles(block):
        return [(o, t) for o in range(3) for t in range(slots(block, o)[0], sum(slots(block, o)))]

    def near(step, o, t):
        _, across, one, two, dev, dev2 = pair(o, t % 2)
        i = (sum(COUNT[:o]) + t) * 3
        sems = [(p1_s.at[i + n], p1_r.at[i + n]) for n in range(3)]
        if step == 0:
            return [
                rcopy(bs[o].at[t, q], r1[o].at[t, n], *sems[n], dev)
                for n, q in ((1, across), (0, one))
            ]
        return two, rcopy(halves[o].at[t], nears[o].at[t], *sems[2], dev2)

    def column(block, o, t):
        return [j for j in range(4) if ORDERS[block][j] == o][t - slots(block, o)[0]]

    def swap(block, o, t):
        i = sum(COUNT[:o]) + t
        mine = gp.at[block - 1, :, pl.ds(128 * column(block, o, t), 128)]
        theirs = yn.at[i]
        return mine, theirs, rcopy(mine, theirs, p1_s.at[3 * i], p1_r.at[3 * i], pair(o, t % 2)[4])

    def near_send(block, columns=(0, 1, 2, 3)):
        for o, t in tiles(block):
            if column(block, o, t) in columns:
                for copy in near(0, o, t) if block < 2 else [swap(block, o, t)[2]]:
                    copy.start()

    came = set()

    def near_pass(block):
        for o, t in tiles(block):
            e = t % 2
            here, _, _, two, _, _ = pair(o, e)
            copy = near(1, o, t)[1]
            if block < 2:
                near(0, o, t)[0].wait_recv()
                halves[o][t] = (bs[o][t, two].astype(F32) + r1[o][t, 1].astype(F32)).astype(BF16)
                copy.start()
                continue
            if (o, e) not in came:
                came.add((o, e))
                for arrival in early(o, e):
                    arrival.wait_recv()
            mine, theirs, swapped = swap(block, o, t)
            swapped.wait_recv()
            for n, q in ((1, two), (0, here)):
                left = quarter(xt, o, q)[...].reshape(256, 256)
                value = dot(left, mine[...]) + dot(xn[o, e, n].reshape(256, 256), theirs[...])
                value = value.astype(BF16).reshape(4, 4, 16, 128)
                into = halves[o].at[t] if n else bs[o].at[t, here]
                if o == 1:
                    for k in range(4):
                        into[:, k] = value[k]
                else:
                    into[...] = value
                if n:
                    copy.start()

    def near_add(block):
        for o, t in tiles(block):
            near(1, o, t)[1].wait_recv()
            value = bs[o][t, coords[o]].astype(F32) + nears[o][t].astype(F32)
            if block < 2:
                near(0, o, t)[1].wait_recv()
                value = value + r1[o][t, 0].astype(F32)
            s1[o][t] = value.astype(BF16)

    def hop(block, o, k):
        there, dev = along((o + 1) % 3, k)
        start, count = slots(block, o)
        at = pl.ds(start, count)
        i = (block * 3 + o) * 3 + k - 1
        return rcopy(s1[o].at[at, there], r2[o].at[k - 1, at], p2_s.at[i], p2_r.at[i], dev)

    def pack():
        for o in range(3):
            for core in range(2):
                for n in range(PAIRS[o]):
                    rows8 = [
                        s2[o][min(i, COUNT[o] - 1), :, 8 * core : 8 * core + 8]
                        for i in (2 * n, 2 * n + 1)
                    ]
                    k2[o][:, core, n] = jnp.concatenate(rows8, axis=1).astype(BF16)

    def last(o, k, rel, sending=True):
        there, dev = along((o + 2) % 3, k)
        i = (o * 4 + k) * 2 + rel
        mine, far = (c, 1 - c) if rel else (c, c)
        dst = r3[o].at[mine if sending else far, k]
        return rcopy(
            k2[o].at[there, far], dst, p3_s.at[i], p3_r.at[i], dev + mate - me if rel else dev
        )

    lasts = [(o, k, rel) for k in (2, 1, 3, 0) for o in range(3) for rel in range(2) if k or rel]

    def far_send(block):
        near_add(block)
        for k in (2, 1, 3):
            for o in range(3):
                hop(block, o, k).start()

    def far_add(block):
        for o in range(3):
            for k in range(1, 4):
                hop(block, o, k).wait_recv()
            start, count = slots(block, o)
            at = slice(start, start + count)
            value = s1[o][at, coords[(o + 1) % 3]].astype(F32)
            for k in range(3):
                value = value + r2[o][k, at].astype(F32)
            s2[o][at] = value

    product(0, gt, ga[...])
    near_send(0)
    product(1, xt, gp[0])
    near_send(1)
    part[0] = dot(ga[...], wo[...], ((1,), (1,))).reshape(2, 2, 64, 1024)

    def across(kind):
        return rcopy(part.at[kind, :, 1 - c], rpart.at[kind], q_s.at[kind], q_r.at[kind], mate)

    def home(kind):
        across(kind).wait_recv()
        mine = pl.multiple_of(64 * c, 64)
        total = [part[kind, o, c] + rpart[kind, o] for o in range(2)]
        if kind:
            for o in range(2):
                total[o] = total[o] + gv[pl.ds(128 * o + mine, 64), :].astype(F32)
        for i in range(4):
            outward(kind, i).wait_send()
        fold(lambda at, cols: total[at.start // 64][:, cols], kind)

    across(0).start()

    for h, o in [(h, o) for h in range(4) for o in range(2)]:
        here = (slice(128 * o, 128 * o + 128), slice(128 * h, 128 * h + 128))
        v, q, k = (act[(f,) + here] for f in (1, 2, 3))
        gmh, w = gm[here], pw[4 * o + h]
        gl = (dot(gmh, v, ((1,), (1,))) * ps[4 * o + h]).astype(BF16)
        grads = (
            dot(w, gmh, ((0,), (0,))),
            dot(gl, k) * scale,
            dot(gl, q, ((0,), (0,))) * scale,
        )
        for f in (1, 2, 3):
            gp[(f,) + here] = (
                grads[f - 1].astype(BF16).astype(F32) * slp[(f,) + here]
            ).astype(BF16)
        if o == 1 and h % 2 == 1:
            for block in range(2, 5):
                near_send(block, (h - 1, h))
    near_pass(0)
    near_pass(1)
    back = dot(gp[0], wi[0], ((1,), (1,)))
    for f in range(1, 4):
        back = back + dot(gp[f], wi[f], ((1,), (1,)))
    part[1] = back.reshape(2, 2, 64, 1024)
    across(1).start()
    near_pass(2)
    near_pass(3)
    near_pass(4)
    far_send(0)
    home(0)
    far_send(1)
    home(1)
    for block in range(2, 5):
        far_send(block)
    scatter(pl.ds(0, 32), rz, z_s, z_r)
    rz[chip] = sa[chip]
    for block in range(5):
        far_add(block)
    pack()
    for step in lasts:
        last(*step).start()
    unpick = jnp.where(to_row(wanted) == rows.astype(F32), 1.0, 0.0).astype(BF16)

    for i in range(4):
        scattered(rz, z_s, z_r, i).wait_recv()

    def returned(kind):
        sf[kind] = rz[:, 16 * kind : 16 * kind + 16].astype(F32).reshape(1024, 128)
        return dot(
            unpick, jnp.concatenate([unfolded(sf.at[kind], o) for o in range(2)], axis=0)
        )

    out[...] = (tok[...].astype(F32) + returned(0)).astype(BF16)
    gx[...] = returned(1).astype(BF16)

    for o, k, rel in lasts:
        last(o, k, rel, False).wait_recv()
    other = pl.multiple_of(512 - half, 512)
    for o in range(3):
        here = coords[(o + 2) % 3]
        for side, base in ((c, half), (1 - c, other)):
            first_term = k2[o][here, c] if base is half else r3[o][side, 0]
            value = first_term.astype(F32)
            for k in range(1, 4):
                value = value + r3[o][side, k].astype(F32)
            for block in range(5):
                for t in range(slots(block, o)[0], sum(slots(block, o))):
                    tile = value[t // 2, 8 * (t % 2) : 8 * (t % 2) + 8]
                    at = 128 * column(block, o, t)
                    if block == 0:
                        gw2[:, pl.ds(base + at, 128)] = tile
                    else:
                        gw1[:, pl.ds((block - 1) * 1024 + base + at, 128)] = tile

    for i in range(4):
        scattered(rz, z_s, z_r, i).wait_send()
        for kind in range(2):
            forward(kind, c, i).wait_send()
    for kind in range(2):
        across(kind).wait_send()
    meta_copy.wait_send()
    stat_copy.wait_send()
    for step in lasts:
        last(*step).wait_send()
    for k in range(1, 4):
        for o in range(3):
            for block in range(5):
                hop(block, o, k).wait_send()
    for block in range(5):
        for o, t in tiles(block):
            near(1, o, t)[1].wait_send()
            for copy in near(0, o, t) if block < 2 else [swap(block, o, t)[2]]:
                copy.wait_send()
    for e in range(2):
        for o in range(3):
            for copy in early(o, e):
                copy.wait_send()


def hand_over(*refs):
    ins, outs, held, (in_sem, out_sem) = refs[:4], refs[4:8], refs[8:12], refs[12:]
    loads = [pltpu.make_async_copy(ins[i], held[i], in_sem.at[i]) for i in range(4)]
    stores = [pltpu.make_async_copy(held[i], outs[i], out_sem.at[i]) for i in range(4)]
    for load in loads:
        load.start()
    for load, store in zip(loads, stores):
        load.wait()
        store.start()
    for store in stores:
        store.wait()


def body(
    tokens, grad_out, w_in, w_out, rel_bias, send_rows, recv_place, block_first, user_rows, stamps
):
    vmem, smem = pl.BlockSpec(memory_space=pltpu.VMEM), pl.BlockSpec(memory_space=pltpu.SMEM)
    hbm = pl.BlockSpec(memory_space=pl.ANY)
    dma = pltpu.SemaphoreType.DMA

    def v(shape, kind=BF16):
        return pltpu.VMEM(shape, kind)

    scratch = [
        v((128, 1024)), v((128, 1024)), pltpu.SMEM((8, 16), F32), v((1, 128), jnp.int32),
        v((1, 128), jnp.int32), v((1, 128), jnp.int32),
        v((4, 1024, 512)), v((1024, 512)), v((2, 1024, 128), F32), v((64, 32, 128)),
        v((2, 2, 64, 16, 128)), v((2, 2, 1024, 128), F32), v((2, 8, 128), F32),
        v((8, 128, 128), F32), v((2, 128, 128), F32), v((256, 1024)), v((256, 1024)),
        v((4, 4, 4, 16, 256)), v((4, 4, 4, 16, 256)), v((4, 256, 512)), v((4, 256, 512), F32),
        v((8, 128, 128)), v((8, 128, 128), F32), v((256, 512), F32), v((256, 512), F32),
        v((2, 256, 128), F32), v((256, 512)), v((256, 512)), v((4, 256, 512)),
    ]
    scratch += [v((n, 4, 4, 4, 16, 128)) for n in COUNT]
    scratch += [v((n, 2, 4, 4, 16, 128)) for n in COUNT]
    scratch += [v((n, 4, 4, 16, 128)) for n in COUNT]
    scratch += [v((n, 4, 4, 16, 128)) for n in COUNT]
    scratch += [v((n, 4, 4, 16, 128)) for n in COUNT]
    scratch += [v((3, n, 4, 16, 128)) for n in COUNT]
    scratch += [v((n, 4, 16, 128), F32) for n in COUNT]
    scratch += [v((2, 4, n, 16, 128)) for n in PAIRS]
    scratch += [v((4, 2, n, 16, 128)) for n in PAIRS]
    scratch += [
        v((2, 2, 2, 64, 1024), F32),
        v((2, 2, 64, 1024), F32), v((64, 32, 128)), v((3, 2, 2, 4, 4, 16, 256)),
        v((20, 256, 128)),
    ]
    scratch += [dma((6,)), dma((5,)), dma((8,)), dma((8,)), dma((8,)), dma((8,))]
    scratch += [dma, dma, dma, dma, dma((60,)), dma((60,)), dma((45,)), dma((45,))]
    scratch += [dma((24,)), dma((24,)), dma((2,)), dma((2,)), dma((4,)), dma((4,))]
    scratch += [dma((12,)), dma((12,))]
    results = pl.pallas_call(
            kernel,
            out_shape=(
                jax.ShapeDtypeStruct((128, 1024), BF16),
                jax.ShapeDtypeStruct((128, 1024), BF16),
                jax.ShapeDtypeStruct((8, 4096), F32),
                jax.ShapeDtypeStruct((8, 1024), F32),
            ),
            in_specs=[hbm] * 7 + [smem, smem, hbm],
            out_specs=(vmem, vmem, vmem, vmem),
            scratch_shapes=scratch,
            compiler_params=pltpu.CompilerParams(
                collective_id=0, has_side_effects=True, vmem_limit_bytes=56 * 2**20
            ),
        )(
            tokens, grad_out, w_in, w_out, rel_bias, send_rows, recv_place, block_first,
            user_rows, stamps.reshape(1, 128),
        )
    return pl.pallas_call(
        hand_over,
        out_shape=tuple(jax.ShapeDtypeStruct(r.shape, r.dtype) for r in results),
        in_specs=[hbm] * 4,
        out_specs=(hbm,) * 4,
        scratch_shapes=[v(r.shape, r.dtype) for r in results] + [dma((4,)), dma((4,))],
    )(*results)


def solution(mesh):
    placed = (
        P("seq", None), P("seq", None), P(), P(), P(), P("seq", None), P("seq", None),
        P("seq"), P("seq"), P("seq"),
    )
    return jax.shard_map(
        body,
        mesh=mesh,
        in_specs=placed,
        out_specs=(P("seq", None), P("seq", None), P("seq", None), P("seq", None)),
        check_vma=False,
    )
```
